512 devices in a mesh: seg: 16 (over z_lo, x), dp: 32 (over y, z_hi, core).
Axes of the slice: x: 4, y: 4, z: 16 (z_hi: 4, z_lo: 4; z = z_hi * 4 + z_lo), core: 2. Of those that a mesh axis runs over, the one named last changes fastest.
Arguments:
- tokens: bfloat16 [16, 32, 128, 4096], P('seg', 'dp'), may hold values from -6 to 6
- cotangent: bfloat16 [16, 32, 128, 4096], P('seg', 'dp'), may hold values from -6 to 6
- query_weight: bfloat16 [4096, 64], P('dp'), may hold values from -0.09375 to 0.09375
- key_weight: bfloat16 [4096, 64], P('dp'), may hold values from -0.09375 to 0.09375
- forget_rate: float32 [16, 32, 64], P('seg', 'dp'), may hold values from 0.003 to 0.6
- resets: int32 [16, 32], P('seg', 'dp'), may hold values 0 or 1
Outputs:
- output: bfloat16 [16, 32, 128, 4096], P('seg', 'dp')
- input_grad: bfloat16 [16, 32, 128, 4096], P('seg', 'dp')
- grad_query: float32 [4096, 64], P(('seg', 'dp'))
- grad_key: float32 [4096, 64], P(('seg', 'dp'))
The draws below stay inside these ranges and needn't reach their ends.
Inputs may be any that keep to these rules, and one draw needn't show every extreme that they name: `resets`: 1 where the segment is the last of its document.
All inputs are finite; a program needn't handle non-finite values. No bound on the sum of `resets` on one device may be relied on, other than what follows from the above.
Results may differ from the reference program's by a relative error of at most 0.0057.
Values may be sent and summed in bfloat16 or wider, within the bound.
A program may use at most 128 MiB of HBM per device.

```python
import math
import jax
import jax.numpy as jnp
from jax import lax

D = 4096
KEY = 64
SEGMENT_TOKENS = 128
SEGS = 16
DOCS = 32


def set_ends(entries, key, least, top_value):
    spot = [jax.random.randint(jax.random.fold_in(key, axis), (), 0, length) for axis, length in enumerate(entries.shape)]
    main_axis = entries.shape.index(max(entries.shape))
    neighbour = spot[:main_axis] + [(spot[main_axis] + 1) % entries.shape[main_axis]] + spot[main_axis + 1:]
    return entries.at[tuple(spot)].set(least).at[tuple(neighbour)].set(top_value)


def spiked(entries, stream_key, source, target, blocks, factor):
    owner, partner = [(jnp.arange(entries.shape[axis_at]) // (entries.shape[axis_at] // blocks)).reshape([-1 if axis == axis_at else 1 for axis in range(entries.ndim)]) for axis_at in (source, target)]
    chosen = jax.random.permutation(stream_key, blocks)[partner]
    strong = (owner == chosen) | (owner == (partner + blocks // 2) % blocks)
    return jnp.where(strong, factor * entries, entries)


def shard_levels(own_key, extent, cuts, least, top_value):
    def one(position, shards_of):
        steps = jax.random.uniform(jax.random.fold_in(jax.random.fold_in(own_key, 6), position), (shards_of,), jnp.float32, least / len(cuts), top_value / len(cuts))
        return jnp.repeat(jnp.exp(steps), extent[position] // shards_of).reshape((-1,) + (1,) * (len(extent) - position - 1))

    gain = one(*cuts[0])
    for cut in cuts[1:]:
        gain = gain * one(*cut)
    return gain


def gaussian(key, dims, scale, bound, split=(), dtype=jnp.bfloat16):
    factor_of = shard_levels(key, dims, split, -0.22, 0.18) if split else 1.0
    result = jax.random.normal(key, dims, jnp.float32) * scale * factor_of
    return jnp.minimum(jnp.maximum(result, -bound), bound).astype(dtype)


def heavy_noise(key, shape, width, limit, pieces, heavy, held_as=jnp.bfloat16):
    drawn = width * jax.random.normal(key, shape, jnp.float32)
    if pieces:
        drawn = drawn * shard_levels(key, shape, pieces, -0.22, 0.18)
    return jnp.clip(spiked(drawn, jax.random.fold_in(key, 3), *heavy), -limit, limit).astype(held_as)


def setup_inputs(seed: int = 0) -> dict:
    splits = jax.random.split(jax.random.key(seed), 7)
    return {
        "tokens": heavy_noise(splits[0], (SEGS, DOCS, SEGMENT_TOKENS, D), 1.0, 6.0, ((0, 16), (1, 32)), (1, 3, 32, 2.75)),
        "cotangent": gaussian(splits[1], (SEGS, DOCS, SEGMENT_TOKENS, D), 1.0, 6.0, ((0, 16), (1, 32))),
        "query_weight": gaussian(splits[2], (D, KEY), D ** -0.5, 0.09375, ((0, 32),)),
        "key_weight": gaussian(splits[3], (D, KEY), D ** -0.5, 0.09375, ((0, 32),)),
        "forget_rate": jnp.clip(jnp.exp(math.log(0.6) - 5.2983174 * jax.random.uniform(splits[4], (SEGS, DOCS, KEY), jnp.float32) ** shard_levels(splits[4], (SEGS, DOCS, KEY), ((0, 16), (1, 32)), -0.2, 0.2)), 0.003, 0.6),
        "resets": set_ends((jax.random.randint(splits[5], (SEGS, DOCS), 0, 8) < 1).astype(jnp.int32), jax.random.fold_in(splits[5], 1), 0, 1),
    }


def feature(values):
    return jnp.where(values > 0, values + 1.0, jnp.exp(jnp.minimum(values, 0.0)))


def feature_slope(values):
    return jnp.where(values > 0, 1.0, jnp.exp(jnp.minimum(values, 0.0)))


def reference(tokens, cotangent, query_weight, key_weight, forget_rate, resets):
    highest_precision = lax.Precision.HIGHEST
    query_full = query_weight.astype(jnp.float32)
    key_full = key_weight.astype(jnp.float32)
    retain_all = jnp.exp(-forget_rate) * (1 - resets).astype(jnp.float32)[:, :, None]
    memory = jnp.zeros((DOCS, KEY, D), jnp.float32)
    memory_list = []
    for segment in range(SEGS):
        input_rows = tokens[segment].astype(jnp.float32)
        keys = jnp.einsum('brd,dk->brk', input_rows, key_full, precision=highest_precision)
        key_features = feature(keys).astype(jnp.bfloat16).astype(jnp.float32)
        memory_update = jnp.einsum('jhp,jhs->jps', key_features, input_rows, precision=highest_precision) / SEGMENT_TOKENS
        memory_list.append(memory)
        memory = retain_all[segment][:, :, None] * memory + memory_update
    carried = jnp.zeros((DOCS, KEY, D), jnp.float32)
    grad_query = jnp.zeros((D, KEY), jnp.float32)
    grad_key = jnp.zeros((D, KEY), jnp.float32)
    outputs = []
    input_grads = []
    for segment in range(SEGS - 1, -1, -1):
        input_rows = tokens[segment].astype(jnp.float32)
        output_gradient = cotangent[segment].astype(jnp.float32)
        queries = jnp.einsum('brd,dk->brk', input_rows, query_full, precision=highest_precision)
        keys = jnp.einsum('brd,dk->brk', input_rows, key_full, precision=highest_precision)
        query_features = feature(queries).astype(jnp.bfloat16).astype(jnp.float32)
        key_features = feature(keys).astype(jnp.bfloat16).astype(jnp.float32)
        memory_readout = memory_list[segment].astype(jnp.bfloat16).astype(jnp.float32)
        output = input_rows + jnp.einsum('ajq,aqw->ajw', query_features, memory_readout, precision=highest_precision)
        outputs.append(output.astype(jnp.bfloat16))
        memory_gradient = jnp.einsum('jhp,jhs->jps', query_features, output_gradient, precision=highest_precision)
        readout_gradient = jnp.einsum('xqo,xwo->xqw', output_gradient, memory_readout, precision=highest_precision)
        query_grad = (readout_gradient * feature_slope(queries)).astype(jnp.bfloat16).astype(jnp.float32)
        update_grad = carried
        update_readout = update_grad.astype(jnp.bfloat16).astype(jnp.float32)
        feature_gradient = jnp.einsum('xqo,xwo->xqw', input_rows, update_readout, precision=highest_precision) / SEGMENT_TOKENS
        key_grad = (feature_gradient * feature_slope(keys)).astype(jnp.bfloat16).astype(jnp.float32)
        writing_gradient = jnp.einsum('ajq,aqw->ajw', key_features, update_readout, precision=highest_precision) / SEGMENT_TOKENS
        project_grad = jnp.einsum('brk,dk->brd', query_grad, query_full, precision=highest_precision) + jnp.einsum('brk,dk->brd', key_grad, key_full, precision=highest_precision)
        input_grads.append((output_gradient + writing_gradient + project_grad).astype(jnp.bfloat16))
        grad_query = grad_query + jnp.einsum('brd,brk->dk', input_rows, query_grad, precision=highest_precision)
        grad_key = grad_key + jnp.einsum('brd,brk->dk', input_rows, key_grad, precision=highest_precision)
        carried = memory_gradient + retain_all[segment][:, :, None] * update_grad
    output_all = jnp.stack(outputs[::-1], axis=0)
    input_grad = jnp.stack(input_grads[::-1], axis=0)
    return output_all, input_grad, grad_query, grad_key
```

```python
import jax
import jax.numpy as jnp
from jax import lax
from jax.experimental import pallas as pl
from jax.experimental.pallas import tpu as pltpu
from jax.sharding import PartitionSpec as P

ZL, X = 4, 4
Y, ZH, C = 4, 4, 2
CHUNKS = 4
KEY = 64
F32 = jnp.float32
BF16 = jnp.bfloat16
MESH = pl.DeviceIdType.MESH


def dot(a, b, ca, cb):
    return lax.dot_general(a, b, (((ca,), (cb,)), ((), ())), preferred_element_type=F32)


def body(
    tok, cot, wq, wk, rate, reset,
    out, igrad, gq, gk,
    w, rt, sin, rin, zs, zr, sb, read, feat, slope, bg,
    gown, gsnd, grcv, hb, r1a, r1b, acc1a, acc1b, h1a, h1b, r2a, r2b, fin, r3,
    a1, a2, a3, a4, rx, rz, s_in, s_z, s_bk, s_c, e1a, e1b, e2a, e2b, e3,
):
    rows, width = tok.shape
    shard = wq.shape[0]
    xs = shard // X
    half = ZL // 2
    wide = width // (CHUNKS * X)
    s = lax.axis_index("seg")
    b = lax.axis_index("dp")
    zl, x = s // X, s % X
    y, zh, c = b // (ZH * C), (b // C) % ZH, b % C

    def dev(zl=zl, x=x, y=y, zh=zh, c=c):
        return (zl * X + x, (y * ZH + zh) * C + c)

    started = []

    def send(src, dst, sem, at, target):
        copy = pltpu.make_async_remote_copy(
            src_ref=src, dst_ref=dst, send_sem=sem.at[(0,) + at], recv_sem=sem.at[(1,) + at],
            device_id=target, device_id_type=MESH,
        )
        copy.start()
        started.append(copy)
        return copy

    w[y, zh, c, :, 0:KEY] = wq[...]
    w[y, zh, c, :, KEY:] = wk[...]
    factor = jnp.exp(-rate[...]) * (1 - reset[...]).astype(F32)
    factor = jnp.concatenate([factor, jnp.zeros_like(factor)], axis=1)
    rt[zl, x] = jnp.broadcast_to(factor, rt.shape[2:])
    zr[:, pl.ds(zl, 1)] = jnp.zeros((zr.shape[0], 1) + zr.shape[2:], BF16)
    zi = zh * ZL + zl
    peers = [dev(x=(x + k) % X) for k in range(1, X)]
    peers += [dev(y=(y + k) % Y) for k in range(1, Y)]
    for k in range(1, ZL * ZH):
        zt = (zi + k) % (ZL * ZH)
        peers.append(dev(zl=zt % ZL, zh=zt // ZL))
    peers.append(dev(c=1 - c))
    barrier = pltpu.get_barrier_semaphore()
    for peer in peers:
        pl.semaphore_signal(barrier, inc=1, device_id=peer, device_id_type=MESH)
    pl.semaphore_wait(barrier, len(peers))

    mine = pl.ds(x * xs, xs)
    part = w.at[y, zh, c, mine]
    got = [send(part, part, a1, (k,), dev(zh=(zh + k) % ZH)) for k in range(1, ZH)]
    own = rt.at[zl, x]
    gotx = [send(own, own, rx, (k,), dev(x=(x + k) % X)) for k in range(1, X)]
    for copy in got:
        copy.wait_recv()
    part = w.at[y, :, c, mine]
    goty = [send(part, part, a2, (k,), dev(y=(y + k) % Y)) for k in range(1, Y)]
    arrived = [[] for _ in range(X)]
    for j in range(Y):
        if j:
            goty[j - 1].wait_recv()
        part = w.at[(y + Y - j) % Y, :, c, mine]
        for k in range(1, X):
            arrived[k].append(send(part, part, a3, (j, k), dev(x=(x + k) % X)))
    cores = []
    for k in range(X):
        for copy in arrived[k]:
            copy.wait_recv()
        part = w.at[:, :, c, pl.ds(((x + X - k) % X) * xs, xs)]
        cores.append(send(part, part, a4, (k,), dev(c=1 - c)))
    for copy in gotx:
        copy.wait_recv()
    own = rt.at[zl]
    gotz = [send(own, own, rz, (k,), dev(zl=(zl + k) % ZL)) for k in range(1, ZL)]
    for copy in cores:
        copy.wait_recv()

    both = dot(tok[...], w[...].reshape(width, 2 * KEY), 1, 0)
    low = jnp.exp(jnp.minimum(both, 0.0))
    features = jnp.where(both > 0, both + 1.0, low)
    slope[...] = jnp.where(both > 0, 1.0, low)
    feat[...] = features.astype(BF16)
    turned = features.T.astype(BF16)

    ins = []
    for j in range(CHUNKS):
        at = slice(j * X * wide, (j + 1) * X * wide)
        update = (dot(turned[KEY:], tok[:, at], 1, 0) / rows).astype(BF16)
        grad = dot(turned[:KEY], cot[:, at], 1, 0).astype(BF16)
        for q in range(X):
            sin[j, q, 0] = update[:, q * wide:(q + 1) * wide]
            sin[j, q, 1] = grad[:, q * wide:(q + 1) * wide]
        ins.append([
            send(sin.at[j, (x + k) % X], rin.at[j, x], s_in, (j, k), dev(x=(x + k) % X))
            for k in range(1, X)
        ])
        rin[j, x] = sin[j, x]

    eye = lax.broadcasted_iota(jnp.int32, (KEY, KEY), 0) == lax.broadcasted_iota(jnp.int32, (KEY, KEY), 1)

    def column(row):
        return jnp.sum(jnp.where(eye, row[0:1, :KEY], 0.0), axis=1, keepdims=True)

    for copy in gotz:
        copy.wait_recv()
    keep = [column(rt[zl, i]) for i in range(X)]
    whole = []
    for z in range(ZL):
        total = column(rt[z, 0])
        for i in range(1, X):
            total = total * column(rt[z, i])
        whole.append(total)
    ahead, behind = [], []
    for z in range(ZL):
        f = jnp.where(z < zl, jnp.ones_like(keep[0]), 0.0)
        for m in range(z + 1, ZL):
            f = f * jnp.where(m < zl, whole[m], 1.0)
        ahead.append(f)
        f = jnp.where(z > zl, jnp.ones_like(keep[0]), 0.0)
        for m in range(z):
            f = f * jnp.where(m > zl, whole[m], 1.0)
        behind.append(f)

    def totals(j):
        for copy in ins[j]:
            copy.wait_recv()
        forward = rin[j, 0, 0].astype(F32)
        backward = rin[j, X - 1, 1].astype(F32)
        for i in range(1, X):
            forward = keep[i] * forward + rin[j, i, 0].astype(F32)
            backward = keep[X - 1 - i] * backward + rin[j, X - 1 - i, 1].astype(F32)
        zs[j, 0] = forward.astype(BF16)
        zs[j, 1] = backward.astype(BF16)
        copies = []
        for k in range(1, ZL):
            zt = (zl + k) % ZL
            way = jnp.where(zt < zl, 1, 0)
            copies.append(send(zs.at[j, way], zr.at[j, zl], s_z, (j, k), dev(zl=zt)))
        return copies

    def finish(j, copies):
        for copy in copies:
            copy.wait_recv()
        forward = jnp.zeros((KEY, wide), F32)
        backward = jnp.zeros((KEY, wide), F32)
        for z in range(ZL):
            block = zr[j, z].astype(F32)
            forward = forward + ahead[z] * block
            backward = backward + behind[z] * block
        for i in range(X):
            sb[j, i, 0] = forward.astype(BF16)
            sb[j, X - 1 - i, 1] = backward.astype(BF16)
            if i < X - 1:
                forward = keep[i] * forward + rin[j, i, 0].astype(F32)
                backward = keep[X - 1 - i] * backward + rin[j, X - 1 - i, 1].astype(F32)
        back = [
            send(sb.at[j, (x + k) % X], read.at[j, x], s_bk, (j, k), dev(x=(x + k) % X))
            for k in range(1, X)
        ]
        read[j, x] = sb[j, x]
        return back

    backs = []
    pending = totals(0)
    for j in range(CHUNKS):
        following = totals(j + 1) if j + 1 < CHUNKS else None
        backs.append(finish(j, pending))
        pending = following

    read_grad = jnp.zeros((rows, KEY), F32)
    feature_grad = jnp.zeros((rows, KEY), F32)
    for j in range(CHUNKS):
        for copy in backs[j]:
            copy.wait_recv()
        for q in range(X):
            at = slice((j * X + q) * wide, (j * X + q + 1) * wide)
            read_grad = read_grad + dot(cot[:, at], read[j, q, 0], 1, 1)
            feature_grad = feature_grad + dot(tok[:, at], read[j, q, 1], 1, 1)
    bg[...] = (jnp.concatenate([read_grad, feature_grad / rows], axis=1) * slope[...]).astype(BF16)

    span = width // ZL
    per = span // (X * Y * ZH * C)
    pair = []
    for z in range(ZL):
        g = dot(tok[:, z * span:(z + 1) * span], bg[...], 0, 0)
        g = g.reshape(X * Y * ZH, C, per, 2 * KEY)
        first = g[:, 0].reshape(X, Y, ZH * per, 2 * KEY)
        second = g[:, 1].reshape(X, Y, ZH * per, 2 * KEY)
        gown[z] = jnp.where(c == 0, first, second)
        gsnd[z] = jnp.where(c == 0, second, first).astype(BF16)
        pair.append(send(gsnd.at[z], grcv.at[z], s_c, (z,), dev(c=1 - c)))
    first_x, first_y = [], []
    for z in range(ZL):
        pair[z].wait_recv()
        total = gown[z] + grcv[z].astype(F32)
        gown[z] = total
        hb[z] = total.astype(BF16)
        if z == half - 1:
            for k in range(1, X):
                xt = (x + k) % X
                first_x.append(send(hb.at[pl.ds(0, half), xt], r1a.at[k], e1a, (k,), dev(x=xt)))
    for k in range(1, Y):
        yt = (y + k) % Y
        first_y.append(send(hb.at[pl.ds(half, half), :, yt], r1b.at[k], e1b, (k,), dev(y=yt)))

    def outputs(j):
        for q in range(X):
            at = slice((j * X + q) * wide, (j * X + q + 1) * wide)
            out[:, at] = (tok[:, at].astype(F32) + dot(feat[:, :KEY], read[j, q, 0], 1, 0)).astype(BF16)

    def input_grads(j):
        for q in range(X):
            n = (j * X + q) * wide
            at = slice(n, n + wide)
            flat = w[...].reshape(width, 2 * KEY)
            total = cot[:, at].astype(F32) + dot(feat[:, KEY:], read[j, q, 1], 1, 0) / rows
            igrad[:, at] = (total + dot(bg[...], flat[n:n + wide], 1, 1)).astype(BF16)

    for j in range(CHUNKS):
        outputs(j)
    for copy in first_x:
        copy.wait_recv()
    total = gown[0:half, x]
    for k in range(1, X):
        total = total + r1a[k].astype(F32)
    acc1a[...] = total
    h1a[...] = total.astype(BF16)
    second_y = []
    for k in range(1, Y):
        yt = (y + k) % Y
        second_y.append(send(h1a.at[:, yt], r2a.at[k], e2a, (k,), dev(y=yt)))
    for copy in first_y:
        copy.wait_recv()
    total = gown[half:, :, y]
    for k in range(1, Y):
        total = total + r1b[k].astype(F32)
    acc1b[...] = total
    h1b[...] = total.astype(BF16)
    second_x = []
    for k in range(1, X):
        xt = (x + k) % X
        second_x.append(send(h1b.at[:, xt], r2b.at[k], e2b, (k,), dev(x=xt)))

    for j in range(CHUNKS // 2):
        input_grads(j)
    for copy in second_y:
        copy.wait_recv()
    total = acc1a[:, y]
    for k in range(1, Y):
        total = total + r2a[k].astype(F32)
    fin[0:half] = total.reshape(half, ZH, per, 2 * KEY)
    for copy in second_x:
        copy.wait_recv()
    total = acc1b[:, x]
    for k in range(1, X):
        total = total + r2b[k].astype(F32)
    fin[half:] = total.reshape(ZL - half, ZH, per, 2 * KEY)
    last = []
    for k in range(1, ZL * ZH):
        zt = (zi + k) % (ZL * ZH)
        last.append(send(fin.at[zt % ZL, zt // ZL], r3.at[k], e3, (k,), dev(zl=zt % ZL, zh=zt // ZL)))

    for j in range(CHUNKS // 2, CHUNKS):
        input_grads(j)
    for copy in last:
        copy.wait_recv()
    total = fin[zl, zh]
    for k in range(1, ZL * ZH):
        total = total + r3[k]
    gq[...] = total[:, :KEY]
    gk[...] = total[:, KEY:]

    for copy in started:
        copy.wait_send()


def local(tokens, cotangent, query_weight, key_weight, forget_rate, resets):
    rows, width = tokens.shape[2:]
    shard = query_weight.shape[0]
    wide = width // (CHUNKS * X)
    half = ZL // 2
    span = width // ZL
    per = span // (X * Y * ZH * C)
    lanes = 2 * KEY
    vm = pltpu.VMEM
    sem = pltpu.SemaphoreType.DMA
    scratch = [
        vm((Y, ZH, C, shard, lanes), BF16),
        vm((ZL, X, 8, lanes), F32),
        vm((CHUNKS, X, 2, KEY, wide), BF16),
        vm((CHUNKS, X, 2, KEY, wide), BF16),
        vm((CHUNKS, 2, KEY, wide), BF16),
        vm((CHUNKS, ZL, KEY, wide), BF16),
        vm((CHUNKS, X, 2, KEY, wide), BF16),
        vm((CHUNKS, X, 2, KEY, wide), BF16),
        vm((rows, lanes), BF16),
        vm((rows, lanes), F32),
        vm((rows, lanes), BF16),
        vm((ZL, X, Y, ZH * per, lanes), F32),
        vm((ZL, X, Y, ZH * per, lanes), BF16),
        vm((ZL, X, Y, ZH * per, lanes), BF16),
        vm((ZL, X, Y, ZH * per, lanes), BF16),
        vm((X, half, Y, ZH * per, lanes), BF16),
        vm((Y, half, X, ZH * per, lanes), BF16),
        vm((half, Y, ZH * per, lanes), F32),
        vm((half, X, ZH * per, lanes), F32),
        vm((half, Y, ZH * per, lanes), BF16),
        vm((half, X, ZH * per, lanes), BF16),
        vm((Y, half, ZH * per, lanes), BF16),
        vm((X, half, ZH * per, lanes), BF16),
        vm((ZL, ZH, per, lanes), F32),
        vm((ZL * ZH, per, lanes), F32),
        sem((2, ZH)), sem((2, Y)), sem((2, Y, X)), sem((2, X)), sem((2, X)), sem((2, ZL)),
        sem((2, CHUNKS, X)), sem((2, CHUNKS, ZL)), sem((2, CHUNKS, X)), sem((2, ZL)),
        sem((2, X)), sem((2, Y)), sem((2, Y)), sem((2, X)), sem((2, ZL * ZH)),
    ]
    whole = pl.BlockSpec(memory_space=pltpu.VMEM)
    output, input_grad, grad_query, grad_key = pl.pallas_call(
        body,
        out_shape=(
            jax.ShapeDtypeStruct((rows, width), BF16),
            jax.ShapeDtypeStruct((rows, width), BF16),
            jax.ShapeDtypeStruct((per, KEY), F32),
            jax.ShapeDtypeStruct((per, KEY), F32),
        ),
        in_specs=[whole] * 6,
        out_specs=(whole,) * 4,
        scratch_shapes=scratch,
        compiler_params=pltpu.CompilerParams(
            collective_id=0, has_side_effects=True, vmem_limit_bytes=48 * 1024 * 1024
        ),
        cost_estimate=pl.CostEstimate(
            flops=16 * rows * width * KEY, bytes_accessed=8 * rows * width, transcendentals=rows * lanes
        ),
    )(tokens[0, 0], cotangent[0, 0], query_weight, key_weight, forget_rate[0], resets)
    return output[None, None], input_grad[None, None], grad_query, grad_key


def solution(mesh):
    placed = (
        P("seg", "dp", None, None),
        P("seg", "dp", None, None),
        P("dp", None),
        P("dp", None),
        P("seg", "dp", None),
        P("seg", "dp"),
    )
    return jax.shard_map(
        local,
        mesh=mesh,
        in_specs=placed,
        out_specs=(
            P("seg", "dp", None, None),
            P("seg", "dp", None, None),
            P(("seg", "dp"), None),
            P(("seg", "dp"), None),
        ),
        check_vma=False,
    )
```

```python
import jax
import jax.numpy as jnp
from jax import lax
from jax.experimental import pallas as pl
from jax.experimental.pallas import tpu as pltpu
from jax.sharding import PartitionSpec as P

ZL, X = 4, 4
Y, ZH, C = 4, 4, 2
CHUNKS = 4
KEY = 64
VMEM_LIMIT = 56 * 1024 * 1024
F32 = jnp.float32
BF16 = jnp.bfloat16
MESH = pl.DeviceIdType.MESH
QUERY, WRITE = 0, 1
FORE, BACK = 0, 1


def dot(a, b, ca, cb):
    return lax.dot_general(a, b, (((ca,), (cb,)), ((), ())), preferred_element_type=F32)


def feature(values):
    return jnp.where(values > 0, values + 1.0, jnp.exp(jnp.minimum(values, 0.0)))


def feature_slope(values):
    return jnp.where(values > 0, 1.0, jnp.exp(jnp.minimum(values, 0.0)))


def body(
    tok_in, cot_in, wq, wk, rate, reset,
    out, igrad, gq, gk,
    tok, cot, tokt, w, rt, sin, rin, zt, zs, zm, za, zb, sb, read, feat, slope, bg,
    gown, gsnd, grcv, hb, r1, fin, r3,
    s_l, s_zs, s_zr, s_y, s_w, s_rx, s_rz, s_in, s_a, s_bs, s_br, s_bk, s_c, s_xy, s_e,
):
    rows, width = tok.shape
    shard = wq.shape[1]
    wide = width // (CHUNKS * X)
    nz = ZL * ZH
    reach = (ZH - 1) * ZL // 2
    s = lax.axis_index("seg")
    b = lax.axis_index("dp")
    zl, x = s // X, s % X
    y, zh, c = b // (ZH * C), (b // C) % ZH, b % C
    zi = zh * ZL + zl

    def dev(zl=zl, x=x, y=y, zh=zh, c=c):
        return (zl * X + x, (y * ZH + zh) * C + c)

    started = []

    def make(src, dst, send_sem, recv_sem, target):
        return pltpu.make_async_remote_copy(
            src_ref=src, dst_ref=dst, send_sem=send_sem, recv_sem=recv_sem,
            device_id=target, device_id_type=MESH,
        )

    def send(src, dst, sem, at, target):
        copy = make(src, dst, sem.at[(0,) + at], sem.at[(1,) + at], target)
        copy.start()
        started.append(copy)
        return copy

    load_tok = pltpu.make_async_copy(tok_in, tok, s_l.at[0])
    load_cot = pltpu.make_async_copy(cot_in, cot, s_l.at[1])
    load_tok.start()
    load_cot.start()
    lanes = pl.ds(pl.multiple_of(c * shard, shard), shard)
    w[QUERY, y, zh, :, lanes] = wq[...]
    w[WRITE, y, zh, :, lanes] = wk[...]
    factor = jnp.exp(-rate[...]) * (1 - reset[...]).astype(F32)
    factor = jnp.concatenate([factor, jnp.zeros_like(factor)], axis=1)
    rt[zl, x] = jnp.broadcast_to(factor, rt.shape[2:])
    za[...] = jnp.zeros_like(za)
    zb[...] = jnp.zeros_like(zb)
    peers = [dev(c=1 - c)]
    peers += [dev(x=(x + k) % X) for k in range(1, X)]
    peers += [dev(y=(y + k) % Y) for k in range(1, Y)]
    peers += [dev(zl=(zl + k) % ZL) for k in range(1, ZL)]
    near = len(peers)
    for o in range(1, ZH):
        peers.append(dev(zl=jnp.where(o * ZL - zl <= reach, 0, ZL - 1), zh=(zh + o) % ZH))
    edge = (zl == 0) | (zl == ZL - 1)
    barrier = pltpu.get_barrier_semaphore()
    for peer in peers:
        pl.semaphore_signal(barrier, inc=1, device_id=peer, device_id_type=MESH)
    pl.semaphore_wait(barrier, near + jnp.where(edge, reach, 0))

    def block(part, o):
        return w.at[part, y, (zh + o) % ZH, :, lanes]

    spread = []
    for part in (WRITE, QUERY):
        for d in range(1, reach + 1):
            zt_ = (zi + jnp.where(zl == 0, -d, d) + nz) % nz
            o = (d - 1) // ZL + 1
            o = jnp.where(zl == 0, o, ZH - o)
            spread.append(make(
                block(part, 0), block(part, 0), s_zs.at[part, d], s_zr.at[part, o],
                dev(zl=zt_ % ZL, zh=zt_ // ZL),
            ))

    @pl.when(edge)
    def _():
        for copy in spread:
            copy.start()

    def arrive_z(part, o):
        make(block(part, o), block(part, o), s_zs.at[part, 0], s_zr.at[part, o], dev(zh=(zh + 1) % ZH)).wait_recv()

    along_y = {}

    def start_y(part, o):
        along_y[part, o] = [
            send(block(part, o), block(part, o), s_y, (part, o, k), dev(y=(y + k) % Y)) for k in range(1, Y)
        ]

    to_core = {WRITE: [], QUERY: []}

    def start_core(part, o):
        for copy in along_y[part, o]:
            copy.wait_recv()
        column = w.at[part, :, (zh + o) % ZH, :, lanes]
        to_core[part].append(send(column, column, s_w, (part, o), dev(c=1 - c)))

    offsets = sorted(range(1, ZH), key=lambda o: min(o, ZH - o))
    start_y(WRITE, 0)
    own = rt.at[zl, x]
    gotx = [send(own, own, s_rx, (k,), dev(x=(x + k) % X)) for k in range(1, X)]
    load_tok.wait()
    step = width // 8
    for n in range(8):
        tokt[n * step:(n + 1) * step] = tok[:, n * step:(n + 1) * step].T
    for copy in gotx:
        copy.wait_recv()
    own = rt.at[zl]
    gotz = [send(own, own, s_rz, (k,), dev(zl=(zl + k) % ZL)) for k in range(1, ZL)]
    load_cot.wait()
    for o in offsets:
        arrive_z(WRITE, o)
        start_y(WRITE, o)
    start_y(QUERY, 0)
    start_core(WRITE, 0)
    for o in offsets:
        arrive_z(QUERY, o)
        start_y(QUERY, o)
        start_core(WRITE, o)
    for copy in to_core[WRITE]:
        copy.wait_recv()

    pairs = [(n // ZH, n % ZH, slice(n * C * shard, (n + 1) * C * shard)) for n in range(Y * ZH)]

    def turned(part):
        total = jnp.zeros((KEY, rows), F32)
        for i, j, at in pairs:
            total = total + dot(w[part, i, j], tok[:, at], 1, 1)
        return feature(total).astype(BF16)

    def straight(part):
        total = jnp.zeros((rows, KEY), F32)
        for i, j, at in pairs:
            total = total + dot(tok[:, at], w[part, i, j], 1, 1)
        feat[part] = feature(total).astype(BF16)
        slope[part] = feature_slope(total)

    ins = {}

    def exchange(way, weights, values, scale):
        for j in range(CHUNKS):
            at = slice(j * X * wide, (j + 1) * X * wide)
            term = (dot(weights, values[:, at], 1, 0) * scale).astype(BF16)
            for q in range(X):
                sin[way, j, q] = term[:, q * wide:(q + 1) * wide]
            ins[way, j] = [
                send(sin.at[way, j, (x + k) % X], rin.at[way, j, x], s_in, (way, j, k), dev(x=(x + k) % X))
                for k in range(1, X)
            ]
            rin[way, j, x] = sin[way, j, x]

    exchange(FORE, turned(WRITE), tok, 1.0 / rows)
    for o in [0] + offsets:
        start_core(QUERY, o)
    for copy in to_core[QUERY]:
        copy.wait_recv()
    exchange(BACK, turned(QUERY), cot, 1.0)

    eye = lax.broadcasted_iota(jnp.int32, (KEY, KEY), 0) == lax.broadcasted_iota(jnp.int32, (KEY, KEY), 1)

    def column(row):
        return jnp.sum(jnp.where(eye, row[0:1, :KEY], 0.0), axis=1, keepdims=True)

    for copy in gotz:
        copy.wait_recv()
    keep = [column(rt[zl, i]) for i in range(X)]
    whole = keep[0]
    for i in range(1, X):
        whole = whole * keep[i]
    place = {FORE: zl, BACK: ZL - 1 - zl}
    ahead = {FORE: 1, BACK: -1}
    order = {FORE: list(range(X)), BACK: list(range(X))[::-1]}
    from_a, from_b = {}, {}
    for way, row in ((FORE, ZL - 2), (BACK, 1)):
        skipped = column(rt[row, 0])
        for i in range(1, X):
            skipped = skipped * column(rt[row, i])
        one = jnp.ones_like(skipped)
        p = place[way]
        from_a[way] = jnp.where(p % 2 == 1, one, 0.0)
        from_b[way] = jnp.where(p == 2, one, jnp.where(p == 3, skipped, 0.0))

    later = []

    def hop(way, steps):
        return dev(zl=(zl + ahead[way] * steps + ZL) % ZL)

    def pass_a(way, j):
        return make(zs.at[way, j], za.at[way, j], s_a.at[0, way, j], s_a.at[1, way, j], hop(way, 1))

    def pass_b(way, j, n):
        return make(zm.at[way, j], zb.at[way, j], s_bs.at[way, j, n], s_br.at[way, j], hop(way, n))

    def totals(way, j):
        for copy in ins[way, j]:
            copy.wait_recv()
        total = rin[way, j, order[way][0]].astype(F32)
        for i in order[way][1:]:
            total = keep[i] * total + rin[way, j, i].astype(F32)
        zt[way, j] = total
        zs[way, j] = total.astype(BF16)

        @pl.when(place[way] % 2 == 0)
        def _():
            pass_a(way, j).start()

    def relay(way, j):
        @pl.when(place[way] == 1)
        def _():
            pass_a(way, j).wait_recv()
            zm[way, j] = (whole * za[way, j].astype(F32) + zt[way, j]).astype(BF16)
            pass_b(way, j, 1).start()
            pass_b(way, j, 2).start()

    backs = {}

    def finish(way, j):
        @pl.when(place[way] >= 2)
        def _():
            pass_b(way, j, 1).wait_recv()

        @pl.when(place[way] == 3)
        def _():
            pass_a(way, j).wait_recv()

        state = from_a[way] * za[way, j].astype(F32) + from_b[way] * zb[way, j].astype(F32)
        for n, i in enumerate(order[way]):
            sb[way, j, i] = state.astype(BF16)
            if n < X - 1:
                state = keep[i] * state + rin[way, j, i].astype(F32)
        backs[way, j] = [
            send(sb.at[way, j, (x + k) % X], read.at[way, j, x], s_bk, (way, j, k), dev(x=(x + k) % X))
            for k in range(1, X)
        ]
        read[way, j, x] = sb[way, j, x]

    plan = [(way, j) for way in (FORE, BACK) for j in range(CHUNKS)]
    for n in range(len(plan) + 2):
        if n < len(plan):
            totals(*plan[n])
        if 1 <= n <= len(plan):
            relay(*plan[n - 1])
        if n >= 2:
            finish(*plan[n - 2])
    straight(QUERY)
    straight(WRITE)

    half = ZL // 2
    span = width // ZL
    per = span // (X * Y * ZH * C)
    blank = jnp.zeros((rows, KEY), BF16)
    pair, plane = {}, {}

    def against(way, values, js):
        total = jnp.zeros((rows, KEY), F32)
        for j in js:
            for copy in backs[way, j]:
                copy.wait_recv()
            for q in range(X):
                at = slice((j * X + q) * wide, (j * X + q + 1) * wide)
                total = total + dot(values[:, at], read[way, j, q], 1, 1)
        return total

    def product(part, grad):
        low = jnp.concatenate([grad, blank], axis=1)
        high = jnp.concatenate([blank, grad], axis=1)
        for z in range(half):
            g = dot(tokt[z * span:(z + 1) * span], low, 1, 0)
            g = g + dot(tokt[(z + half) * span:(z + half + 1) * span], high, 1, 0)
            g = g.reshape(X * Y * ZH, C, per, 2 * KEY)
            first = g[:, 0].reshape(X, Y, ZH * per, 2 * KEY)
            second = g[:, 1].reshape(X, Y, ZH * per, 2 * KEY)
            gown[part, z] = jnp.where(c == 0, first, second)
            gsnd[part, z] = jnp.where(c == 0, second, first).astype(BF16)
            pair[part, z] = send(gsnd.at[part, z], grcv.at[part, z], s_c, (part, z), dev(c=1 - c))

    def over_plane(part):
        for z in range(half):
            pair[part, z].wait_recv()
            total = gown[part, z] + grcv[part, z].astype(F32)
            gown[part, z] = total
            hb[part, z] = total.astype(BF16)
        plane[part] = []
        for k in range(1, X * Y):
            xt, yt = (x + k // Y) % X, (y + k % Y) % Y
            plane[part].append(send(hb.at[part, :, xt, yt], r1.at[part, k], s_xy, (part, k), dev(x=xt, y=yt)))

    def gather_plane(part):
        for copy in plane[part]:
            copy.wait_recv()
        total = gown[part, :, x, y]
        for k in range(1, X * Y):
            total = total + r1[part, k].astype(F32)
        for h in range(2):
            piece = total[:, :, h * KEY:(h + 1) * KEY].reshape(half, ZH, per, KEY)
            fin[h * half:(h + 1) * half, :, :, part * KEY:(part + 1) * KEY] = piece

    query_grad = (against(FORE, cot, range(CHUNKS)) * slope[QUERY]).astype(BF16)
    bg[QUERY] = query_grad
    product(QUERY, query_grad)
    wanted = against(BACK, tok, range(CHUNKS - 1))
    over_plane(QUERY)
    wanted = wanted + against(BACK, tok, range(CHUNKS - 1, CHUNKS))
    key_grad = (wanted / rows * slope[WRITE]).astype(BF16)
    bg[WRITE] = key_grad
    product(WRITE, key_grad)
    over_plane(WRITE)

    for j in range(CHUNKS):
        for q in range(X):
            at = slice((j * X + q) * wide, (j * X + q + 1) * wide)
            out[:, at] = (tok[:, at].astype(F32) + dot(feat[QUERY], read[FORE, j, q], 1, 0)).astype(BF16)
    gather_plane(QUERY)
    gather_plane(WRITE)
    last = []
    for k in range(1, nz):
        zt_ = (zi + k) % nz
        last.append(send(fin.at[zt_ % ZL, zt_ // ZL], r3.at[k], s_e, (k,), dev(zl=zt_ % ZL, zh=zt_ // ZL)))

    for j in range(CHUNKS):
        for q in range(X):
            n = (j * X + q) * wide
            at = slice(n, n + wide)
            i, m, n = n // (ZH * C * shard), n // (C * shard) % ZH, n % (C * shard)
            total = cot[:, at].astype(F32) + dot(feat[WRITE], read[BACK, j, q], 1, 0) / rows
            for part in (QUERY, WRITE):
                total = total + dot(bg[part], w[part, i, m, :, n:n + wide], 1, 0)
            igrad[:, at] = total.astype(BF16)
    for copy in last:
        copy.wait_recv()
    total = fin[zl, zh]
    for k in range(1, nz):
        total = total + r3[k]
    gq[...] = total[:, :KEY]
    gk[...] = total[:, KEY:]

    for copy in started:
        copy.wait_send()

    @pl.when(edge)
    def _():
        for copy in spread:
            copy.wait_send()

    for way, j in plan:
        @pl.when(place[way] % 2 == 0)
        def _():
            pass_a(way, j).wait_send()

        @pl.when(place[way] == 1)
        def _():
            pass_b(way, j, 1).wait_send()
            pass_b(way, j, 2).wait_send()


def publish(*refs):
    n = len(refs) // 3
    sem = refs[-1]
    inward = [pltpu.make_async_copy(refs[i], refs[2 * n + i], sem.at[0, i]) for i in range(n)]
    outward = [pltpu.make_async_copy(refs[2 * n + i], refs[n + i], sem.at[1, i]) for i in range(n)]
    for copy in inward:
        copy.start()
    for i in range(n):
        inward[i].wait()
        outward[i].start()
    for copy in outward:
        copy.wait()


def local(tokens, cotangent, query_weight, key_weight, forget_rate, resets):
    rows, width = tokens.shape[2:]
    shard = query_weight.shape[0]
    wide = width // (CHUNKS * X)
    half = ZL // 2
    span = width // ZL
    per = span // (X * Y * ZH * C)
    nz = ZL * ZH
    reach = (ZH - 1) * ZL // 2
    lanes = 2 * KEY
    vm = pltpu.VMEM
    sem = pltpu.SemaphoreType.DMA
    scratch = [
        vm((rows, width), BF16),
        vm((rows, width), BF16),
        vm((width, rows), BF16),
        vm((2, Y, ZH, KEY, C * shard), BF16),
        vm((ZL, X, 8, lanes), F32),
        vm((2, CHUNKS, X, KEY, wide), BF16),
        vm((2, CHUNKS, X, KEY, wide), BF16),
        vm((2, CHUNKS, KEY, wide), F32),
        vm((2, CHUNKS, KEY, wide), BF16),
        vm((2, CHUNKS, KEY, wide), BF16),
        vm((2, CHUNKS, KEY, wide), BF16),
        vm((2, CHUNKS, KEY, wide), BF16),
        vm((2, CHUNKS, X, KEY, wide), BF16),
        vm((2, CHUNKS, X, KEY, wide), BF16),
        vm((2, rows, KEY), BF16),
        vm((2, rows, KEY), F32),
        vm((2, rows, KEY), BF16),
        vm((2, half, X, Y, ZH * per, lanes), F32),
        vm((2, half, X, Y, ZH * per, lanes), BF16),
        vm((2, half, X, Y, ZH * per, lanes), BF16),
        vm((2, half, X, Y, ZH * per, lanes), BF16),
        vm((2, X * Y, half, ZH * per, lanes), BF16),
        vm((ZL, ZH, per, lanes), F32),
        vm((nz, per, lanes), F32),
        sem((2,)), sem((2, reach + 1)), sem((2, ZH)), sem((2, 2, ZH, Y)), sem((2, 2, ZH)),
        sem((2, X)), sem((2, ZL)), sem((2, 2, CHUNKS, X)), sem((2, 2, CHUNKS)),
        sem((2, CHUNKS, 3)), sem((2, CHUNKS)), sem((2, 2, CHUNKS, X)), sem((2, 2, half)),
        sem((2, 2, X * Y)), sem((2, nz)),
    ]
    whole = pl.BlockSpec(memory_space=pltpu.VMEM)
    anywhere = pl.BlockSpec(memory_space=pl.ANY)
    shapes = (
        jax.ShapeDtypeStruct((rows, width), BF16),
        jax.ShapeDtypeStruct((rows, width), BF16),
        jax.ShapeDtypeStruct((per, KEY), F32),
        jax.ShapeDtypeStruct((per, KEY), F32),
    )
    results = pl.pallas_call(
        body,
        out_shape=shapes,
        in_specs=[anywhere] * 2 + [whole] * 4,
        out_specs=(whole,) * 4,
        scratch_shapes=scratch,
        compiler_params=pltpu.CompilerParams(
            collective_id=0, has_side_effects=True, vmem_limit_bytes=VMEM_LIMIT
        ),
        cost_estimate=pl.CostEstimate(
            flops=16 * rows * width * KEY, bytes_accessed=8 * rows * width, transcendentals=rows * lanes
        ),
    )(tokens[0, 0], cotangent[0, 0], query_weight.T, key_weight.T, forget_rate[0], resets)
    output, input_grad, grad_query, grad_key = pl.pallas_call(
        publish,
        out_shape=shapes,
        in_specs=[anywhere] * 4,
        out_specs=(anywhere,) * 4,
        scratch_shapes=[vm(r.shape, r.dtype) for r in shapes] + [sem((2, 4))],
        compiler_params=pltpu.CompilerParams(vmem_limit_bytes=VMEM_LIMIT),
    )(*results)
    return output[None, None], input_grad[None, None], grad_query, grad_key


def solution(mesh):
    placed = (
        P("seg", "dp", None, None),
        P("seg", "dp", None, None),
        P("dp", None),
        P("dp", None),
        P("seg", "dp", None),
        P("seg", "dp"),
    )
    return jax.shard_map(
        local,
        mesh=mesh,
        in_specs=placed,
        out_specs=(
            P("seg", "dp", None, None),
            P("seg", "dp", None, None),
            P(("seg", "dp"), None),
            P(("seg", "dp"), None),
        ),
        check_vma=False,
    )
```

```python
import jax
import jax.numpy as jnp
from jax import lax
from jax.experimental import pallas as pl
from jax.experimental.pallas import tpu as pltpu
from jax.sharding import PartitionSpec as P

ZL, X = 4, 4
Y, ZH, C = 4, 4, 2
CHUNKS = 4
KEY = 64
PIECES = 4
VMEM_LIMIT = 56 * 1024 * 1024
F32 = jnp.float32
BF16 = jnp.bfloat16
MESH = pl.DeviceIdType.MESH
QUERY, WRITE = 0, 1
FORE, BACK = 0, 1


def dot(a, b, ca, cb):
    return lax.dot_general(a, b, (((ca,), (cb,)), ((), ())), preferred_element_type=F32)


def feature(values):
    return jnp.where(values > 0, values + 1.0, jnp.exp(jnp.minimum(values, 0.0)))


def feature_slope(values):
    return jnp.where(values > 0, 1.0, jnp.exp(jnp.minimum(values, 0.0)))


def body(
    tok_in, cot_in, wq_in, wk_in, rate_in, reset_in,
    out_to, igrad_to, gq_to, gk_to,
    tok, cot, wq, wk, rate, reset, out, igrad, gq, gk, tokt, w, rt, sin, rin, zt, zs, zm, za, zb, sb, read, feat, slope, bg,
    gown, gsnd, grcv, hb, r1, fin, r3,
    s_l, s_s, s_zs, s_zr, s_y, s_w, s_rx, s_rz, s_in, s_a, s_bs, s_br, s_bk, s_c, s_xy, s_e,
):
    rows, width = tok.shape
    shard = wq.shape[1]
    wide = width // (CHUNKS * X)
    nz = ZL * ZH
    reach = (ZH - 1) * ZL // 2
    s = lax.axis_index("seg")
    b = lax.axis_index("dp")
    zl, x = s // X, s % X
    y, zh, c = b // (ZH * C), (b // C) % ZH, b % C
    zi = zh * ZL + zl

    def dev(zl=zl, x=x, y=y, zh=zh, c=c):
        return (zl * X + x, (y * ZH + zh) * C + c)

    started = []

    def make(src, dst, send_sem, recv_sem, target):
        return pltpu.make_async_remote_copy(
            src_ref=src, dst_ref=dst, send_sem=send_sem, recv_sem=recv_sem,
            device_id=target, device_id_type=MESH,
        )

    def send(src, dst, sem, at, target):
        copy = make(src, dst, sem.at[(0,) + at], sem.at[(1,) + at], target)
        copy.start()
        started.append(copy)
        return copy

    moves = ((wk_in, wk), (wq_in, wq), (rate_in, rate), (reset_in, reset), (tok_in, tok), (cot_in, cot))
    loads = [pltpu.make_async_copy(src, dst, s_l.at[i]) for i, (src, dst) in enumerate(moves)]
    for copy in loads:
        copy.start()
    za[...] = jnp.zeros_like(za)
    zb[...] = jnp.zeros_like(zb)
    peers = [dev(c=1 - c)]
    peers += [dev(x=(x + k) % X) for k in range(1, X)]
    peers += [dev(y=(y + k) % Y) for k in range(1, Y)]
    peers += [dev(zl=(zl + k) % ZL) for k in range(1, ZL)]
    near = len(peers)
    for o in range(1, ZH):
        peers.append(dev(zl=jnp.where(o * ZL - zl <= reach, 0, ZL - 1), zh=(zh + o) % ZH))
    edge = (zl == 0) | (zl == ZL - 1)
    barrier = pltpu.get_barrier_semaphore()
    for peer in peers:
        pl.semaphore_signal(barrier, inc=1, device_id=peer, device_id_type=MESH)
    for copy in loads[:4]:
        copy.wait()
    lanes = pl.ds(pl.multiple_of(c * shard, shard), shard)
    w[QUERY, y, zh, :, lanes] = wq[...]
    w[WRITE, y, zh, :, lanes] = wk[...]
    factor = jnp.exp(-rate[...]) * (1 - reset[...]).astype(F32)
    factor = jnp.concatenate([factor, jnp.zeros_like(factor)], axis=1)
    rt[zl, x] = jnp.broadcast_to(factor, rt.shape[2:])
    pl.semaphore_wait(barrier, near + jnp.where(edge, reach, 0))

    def block(part, o):
        return w.at[part, y, (zh + o) % ZH, :, lanes]

    spread = []
    for part in (WRITE, QUERY):
        for d in range(reach, 0, -1):
            zt_ = (zi + jnp.where(zl == 0, -d, d) + nz) % nz
            o = (d - 1) // ZL + 1
            o = jnp.where(zl == 0, o, ZH - o)
            spread.append(make(
                block(part, 0), block(part, 0), s_zs.at[part, d], s_zr.at[part, o],
                dev(zl=zt_ % ZL, zh=zt_ // ZL),
            ))

    @pl.when(edge)
    def _():
        for copy in spread:
            copy.start()

    def arrive_z(part, o):
        make(block(part, o), block(part, o), s_zs.at[part, 0], s_zr.at[part, o], dev(zh=(zh + 1) % ZH)).wait_recv()

    along_y = {}

    def start_y(part, o):
        along_y[part, o] = [
            send(block(part, o), block(part, o), s_y, (part, o, k), dev(y=(y + k) % Y)) for k in range(1, Y)
        ]

    to_core = {WRITE: [], QUERY: []}

    def start_core(part, o):
        for copy in along_y[part, o]:
            copy.wait_recv()
        column = w.at[part, :, (zh + o) % ZH, :, lanes]
        to_core[part].append(send(column, column, s_w, (part, o), dev(c=1 - c)))

    offsets = sorted(range(1, ZH), key=lambda o: min(o, ZH - o))
    start_y(WRITE, 0)
    own = rt.at[zl, x]
    gotx = [send(own, own, s_rx, (k,), dev(x=(x + k) % X)) for k in range(1, X)]
    loads[4].wait()
    step = width // 8
    for n in range(8):
        tokt[n * step:(n + 1) * step] = tok[:, n * step:(n + 1) * step].T
    for copy in gotx:
        copy.wait_recv()
    own = rt.at[zl]
    gotz = [send(own, own, s_rz, (k,), dev(zl=(zl + k) % ZL)) for k in range(1, ZL)]
    loads[5].wait()
    for o in offsets:
        arrive_z(WRITE, o)
        start_y(WRITE, o)
    start_y(QUERY, 0)
    start_core(WRITE, 0)
    for o in offsets:
        arrive_z(QUERY, o)
        start_y(QUERY, o)
        start_core(WRITE, o)
    for copy in to_core[WRITE]:
        copy.wait_recv()

    pairs = [(n // ZH, n % ZH, slice(n * C * shard, (n + 1) * C * shard)) for n in range(Y * ZH)]

    def turned(part):
        total = jnp.zeros((KEY, rows), F32)
        for i, j, at in pairs:
            total = total + dot(w[part, i, j], tok[:, at], 1, 1)
        return feature(total).astype(BF16)

    def straight(part):
        total = jnp.zeros((rows, KEY), F32)
        for i, j, at in pairs:
            total = total + dot(tok[:, at], w[part, i, j], 1, 1)
        feat[part] = feature(total).astype(BF16)
        slope[part] = feature_slope(total)

    ins = {}

    def exchange(way, weights, values, scale):
        for j in range(CHUNKS):
            at = slice(j * X * wide, (j + 1) * X * wide)
            term = (dot(weights, values[:, at], 1, 0) * scale).astype(BF16)
            for q in range(X):
                sin[way, j, q] = term[:, q * wide:(q + 1) * wide]
            ins[way, j] = [
                send(sin.at[way, j, (x + k) % X], rin.at[way, j, x], s_in, (way, j, k), dev(x=(x + k) % X))
                for k in range(1, X)
            ]
            rin[way, j, x] = sin[way, j, x]

    exchange(FORE, turned(WRITE), tok, 1.0 / rows)
    straight(WRITE)
    for o in [0] + offsets:
        start_core(QUERY, o)
    for copy in to_core[QUERY]:
        copy.wait_recv()
    exchange(BACK, turned(QUERY), cot, 1.0)
    straight(QUERY)

    eye = lax.broadcasted_iota(jnp.int32, (KEY, KEY), 0) == lax.broadcasted_iota(jnp.int32, (KEY, KEY), 1)

    def column(row):
        return jnp.sum(jnp.where(eye, row[0:1, :KEY], 0.0), axis=1, keepdims=True)

    for copy in gotz:
        copy.wait_recv()
    keep = [column(rt[zl, i]) for i in range(X)]
    whole = keep[0]
    for i in range(1, X):
        whole = whole * keep[i]
    place = {FORE: zl, BACK: ZL - 1 - zl}
    ahead = {FORE: 1, BACK: -1}
    order = {FORE: list(range(X)), BACK: list(range(X))[::-1]}
    from_a, from_b = {}, {}
    for way, row in ((FORE, ZL - 2), (BACK, 1)):
        skipped = column(rt[row, 0])
        for i in range(1, X):
            skipped = skipped * column(rt[row, i])
        one = jnp.ones_like(skipped)
        p = place[way]
        from_a[way] = jnp.where(p % 2 == 1, one, 0.0)
        from_b[way] = jnp.where(p == 2, one, jnp.where(p == 3, skipped, 0.0))

    later = []

    def hop(way, steps):
        return dev(zl=(zl + ahead[way] * steps + ZL) % ZL)

    def pass_a(way, j):
        return make(zs.at[way, j], za.at[way, j], s_a.at[0, way, j], s_a.at[1, way, j], hop(way, 1))

    def pass_b(way, j, n):
        return make(zm.at[way, j], zb.at[way, j], s_bs.at[way, j, n], s_br.at[way, j], hop(way, n))

    def totals(way, j):
        for copy in ins[way, j]:
            copy.wait_recv()
        total = rin[way, j, order[way][0]].astype(F32)
        for i in order[way][1:]:
            total = keep[i] * total + rin[way, j, i].astype(F32)
        zt[way, j] = total
        zs[way, j] = total.astype(BF16)

        @pl.when(place[way] % 2 == 0)
        def _():
            pass_a(way, j).start()

    def relay(way, j):
        @pl.when(place[way] == 1)
        def _():
            pass_a(way, j).wait_recv()
            zm[way, j] = (whole * za[way, j].astype(F32) + zt[way, j]).astype(BF16)
            pass_b(way, j, 1).start()
            pass_b(way, j, 2).start()

    backs = {}

    def finish(way, j):
        @pl.when(place[way] >= 2)
        def _():
            pass_b(way, j, 1).wait_recv()

        @pl.when(place[way] == 3)
        def _():
            pass_a(way, j).wait_recv()

        state = from_a[way] * za[way, j].astype(F32) + from_b[way] * zb[way, j].astype(F32)
        for n, i in enumerate(order[way]):
            sb[way, j, i] = state.astype(BF16)
            if n < X - 1:
                state = keep[i] * state + rin[way, j, i].astype(F32)
        backs[way, j] = [
            send(sb.at[way, j, (x + k) % X], read.at[way, j, x], s_bk, (way, j, k), dev(x=(x + k) % X))
            for k in range(1, X)
        ]
        read[way, j, x] = sb[way, j, x]

    plan = [(way, j) for way in (FORE, BACK) for j in range(CHUNKS)]
    for n in range(len(plan) + 2):
        if n < len(plan):
            totals(*plan[n])
        if 1 <= n <= len(plan):
            relay(*plan[n - 1])
        if n >= 2:
            finish(*plan[n - 2])

    half = ZL // 2
    span = width // ZL
    per = span // (X * Y * ZH * C)
    blank = jnp.zeros((rows, KEY), BF16)
    pair, plane = {}, {}

    def against(way, values, js):
        total = jnp.zeros((rows, KEY), F32)
        for j in js:
            for copy in backs[way, j]:
                copy.wait_recv()
            for q in range(X):
                at = slice((j * X + q) * wide, (j * X + q + 1) * wide)
                total = total + dot(values[:, at], read[way, j, q], 1, 1)
        return total

    def product(part, grad):
        low = jnp.concatenate([grad, blank], axis=1)
        high = jnp.concatenate([blank, grad], axis=1)
        for z in range(half):
            g = dot(tokt[z * span:(z + 1) * span], low, 1, 0)
            g = g + dot(tokt[(z + half) * span:(z + half + 1) * span], high, 1, 0)
            g = g.reshape(X * Y * ZH, C, per, 2 * KEY)
            first = g[:, 0].reshape(X, Y, ZH * per, 2 * KEY)
            second = g[:, 1].reshape(X, Y, ZH * per, 2 * KEY)
            gown[part, z] = jnp.where(c == 0, first, second)
            gsnd[part, z] = jnp.where(c == 0, second, first).astype(BF16)
            pair[part, z] = send(gsnd.at[part, z], grcv.at[part, z], s_c, (part, z), dev(c=1 - c))

    def over_plane(part):
        for z in range(half):
            pair[part, z].wait_recv()
            total = gown[part, z] + grcv[part, z].astype(F32)
            gown[part, z] = total
            hb[part, z] = total.astype(BF16)
        plane[part] = []
        for k in sorted(range(1, X * Y), key=lambda k: -min(k // Y, X - k // Y) - min(k % Y, Y - k % Y)):
            xt, yt = (x + k // Y) % X, (y + k % Y) % Y
            plane[part].append(send(hb.at[part, :, xt, yt], r1.at[part, k], s_xy, (part, k), dev(x=xt, y=yt)))

    def gather_plane(part):
        for copy in plane[part]:
            copy.wait_recv()
        total = gown[part, :, x, y]
        for k in range(1, X * Y):
            total = total + r1[part, k].astype(F32)
        for h in range(2):
            piece = total[:, :, h * KEY:(h + 1) * KEY].reshape(half, ZH, per, KEY)
            fin[h * half:(h + 1) * half, :, :, part * KEY:(part + 1) * KEY] = piece

    query_grad = (against(FORE, cot, range(CHUNKS)) * slope[QUERY]).astype(BF16)
    bg[QUERY] = query_grad
    product(QUERY, query_grad)
    wanted = against(BACK, tok, range(CHUNKS - 1))
    over_plane(QUERY)
    wanted = wanted + against(BACK, tok, range(CHUNKS - 1, CHUNKS))
    key_grad = (wanted / rows * slope[WRITE]).astype(BF16)
    bg[WRITE] = key_grad
    product(WRITE, key_grad)
    over_plane(WRITE)

    for j in range(CHUNKS):
        for q in range(X):
            at = slice((j * X + q) * wide, (j * X + q + 1) * wide)
            out[:, at] = (tok[:, at].astype(F32) + dot(feat[QUERY], read[FORE, j, q], 1, 0)).astype(BF16)
    stores = [pltpu.make_async_copy(out, out_to, s_s.at[0])]
    stores[0].start()
    gather_plane(QUERY)
    gather_plane(WRITE)
    last = []
    for k in sorted(range(1, nz), key=lambda k: -min(k, nz - k)):
        zt_ = (zi + k) % nz
        last.append(send(fin.at[zt_ % ZL, zt_ // ZL], r3.at[k], s_e, (k,), dev(zl=zt_ % ZL, zh=zt_ // ZL)))

    for j in range(CHUNKS):
        for q in range(X):
            n = (j * X + q) * wide
            at = slice(n, n + wide)
            i, m, n = n // (ZH * C * shard), n // (C * shard) % ZH, n % (C * shard)
            total = cot[:, at].astype(F32) + dot(feat[WRITE], read[BACK, j, q], 1, 0) / rows
            for part in (QUERY, WRITE):
                total = total + dot(bg[part], w[part, i, m, :, n:n + wide], 1, 0)
            igrad[:, at] = total.astype(BF16)
    stores.append(pltpu.make_async_copy(igrad, igrad_to, s_s.at[1]))
    stores[1].start()
    for copy in last:
        copy.wait_recv()
    total = fin[zl, zh]
    for k in range(1, nz):
        total = total + r3[k]
    gq[...] = total[:, :KEY]
    gk[...] = total[:, KEY:]
    for i, (src, dst) in enumerate(((gq, gq_to), (gk, gk_to))):
        stores.append(pltpu.make_async_copy(src, dst, s_s.at[2 + i]))
        stores[-1].start()

    for copy in stores:
        copy.wait()
    for copy in started:
        copy.wait_send()

    @pl.when(edge)
    def _():
        for copy in spread:
            copy.wait_send()

    for way, j in plan:
        @pl.when(place[way] % 2 == 0)
        def _():
            pass_a(way, j).wait_send()

        @pl.when(place[way] == 1)
        def _():
            pass_b(way, j, 1).wait_send()
            pass_b(way, j, 2).wait_send()


def publish(*refs):
    sem = refs[-1]
    pieces = []
    for src, dst, held in zip(refs[:4], refs[4:8], refs[8:12]):
        n = PIECES if src.shape[0] % (16 * PIECES) == 0 else 1
        m = src.shape[0] // n
        pieces += [tuple(ref.at[pl.ds(i * m, m)] for ref in (src, held, dst)) for i in range(n)]
    inward, outward = [], []
    for i, (src, held, dst) in enumerate(pieces):
        inward.append(pltpu.make_async_copy(src, held, sem.at[0, i]))
        outward.append(pltpu.make_async_copy(held, dst, sem.at[1, i]))
        inward[-1].start()
    for copy, following in zip(inward, outward):
        copy.wait()
        following.start()
    for copy in outward:
        copy.wait()


def local(tokens, cotangent, query_weight, key_weight, forget_rate, resets):
    rows, width = tokens.shape[2:]
    shard = query_weight.shape[0]
    wide = width // (CHUNKS * X)
    half = ZL // 2
    span = width // ZL
    per = span // (X * Y * ZH * C)
    nz = ZL * ZH
    reach = (ZH - 1) * ZL // 2
    lanes = 2 * KEY
    vm = pltpu.VMEM
    sem = pltpu.SemaphoreType.DMA
    scratch = [
        vm((rows, width), BF16),
        vm((rows, width), BF16),
        vm((KEY, shard), BF16),
        vm((KEY, shard), BF16),
        vm((1, KEY), F32),
        vm((1, 1), jnp.int32),
        vm((rows, width), BF16),
        vm((rows, width), BF16),
        vm((per, KEY), F32),
        vm((per, KEY), F32),
        vm((width, rows), BF16),
        vm((2, Y, ZH, KEY, C * shard), BF16),
        vm((ZL, X, 8, lanes), F32),
        vm((2, CHUNKS, X, KEY, wide), BF16),
        vm((2, CHUNKS, X, KEY, wide), BF16),
        vm((2, CHUNKS, KEY, wide), F32),
        vm((2, CHUNKS, KEY, wide), BF16),
        vm((2, CHUNKS, KEY, wide), BF16),
        vm((2, CHUNKS, KEY, wide), BF16),
        vm((2, CHUNKS, KEY, wide), BF16),
        vm((2, CHUNKS, X, KEY, wide), BF16),
        vm((2, CHUNKS, X, KEY, wide), BF16),
        vm((2, rows, KEY), BF16),
        vm((2, rows, KEY), F32),
        vm((2, rows, KEY), BF16),
        vm((2, half, X, Y, ZH * per, lanes), F32),
        vm((2, half, X, Y, ZH * per, lanes), BF16),
        vm((2, half, X, Y, ZH * per, lanes), BF16),
        vm((2, half, X, Y, ZH * per, lanes), BF16),
        vm((2, X * Y, half, ZH * per, lanes), BF16),
        vm((ZL, ZH, per, lanes), F32),
        vm((nz, per, lanes), F32),
        sem((6,)), sem((4,)), sem((2, reach + 1)), sem((2, ZH)), sem((2, 2, ZH, Y)), sem((2, 2, ZH)),
        sem((2, X)), sem((2, ZL)), sem((2, 2, CHUNKS, X)), sem((2, 2, CHUNKS)),
        sem((2, CHUNKS, 3)), sem((2, CHUNKS)), sem((2, 2, CHUNKS, X)), sem((2, 2, half)),
        sem((2, 2, X * Y)), sem((2, nz)),
    ]
    anywhere = pl.BlockSpec(memory_space=pl.ANY)
    shapes = (
        jax.ShapeDtypeStruct((rows, width), BF16),
        jax.ShapeDtypeStruct((rows, width), BF16),
        jax.ShapeDtypeStruct((per, KEY), F32),
        jax.ShapeDtypeStruct((per, KEY), F32),
    )
    results = pl.pallas_call(
        body,
        out_shape=shapes,
        in_specs=[anywhere] * 6,
        out_specs=(anywhere,) * 4,
        scratch_shapes=scratch,
        compiler_params=pltpu.CompilerParams(
            collective_id=0, has_side_effects=True, vmem_limit_bytes=VMEM_LIMIT
        ),
        cost_estimate=pl.CostEstimate(
            flops=16 * rows * width * KEY, bytes_accessed=8 * rows * width, transcendentals=rows * lanes
        ),
    )(tokens[0, 0], cotangent[0, 0], query_weight.T, key_weight.T, forget_rate[0], resets)
    output, input_grad, grad_query, grad_key = pl.pallas_call(
        publish,
        out_shape=shapes,
        in_specs=[anywhere] * 4,
        out_specs=(anywhere,) * 4,
        scratch_shapes=[vm(r.shape, r.dtype) for r in shapes] + [sem((2, 2 * PIECES + 2))],
        compiler_params=pltpu.CompilerParams(vmem_limit_bytes=VMEM_LIMIT),
    )(*results)
    return output[None, None], input_grad[None, None], grad_query, grad_key


def solution(mesh):
    placed = (
        P("seg", "dp", None, None),
        P("seg", "dp", None, None),
        P("dp", None),
        P("dp", None),
        P("seg", "dp", None),
        P("seg", "dp"),
    )
    return jax.shard_map(
        local,
        mesh=mesh,
        in_specs=placed,
        out_specs=(
            P("seg", "dp", None, None),
            P("seg", "dp", None, None),
            P(("seg", "dp"), None),
            P(("seg", "dp"), None),
        ),
        check_vma=False,
    )
```

```python
import jax
import jax.numpy as jnp
from jax import lax
from jax.experimental import pallas as pl
from jax.experimental.pallas import tpu as pltpu
from jax.sharding import PartitionSpec as P

ZL, X = 4, 4
Y, ZH, C = 4, 4, 2
CHUNKS = 2
KEY = 64
VMEM_LIMIT = 56 * 1024 * 1024
F32 = jnp.float32
BF16 = jnp.bfloat16
MESH = pl.DeviceIdType.MESH
QUERY, WRITE = 0, 1
FORE, BACK = 0, 1


def dot(a, b, ca, cb):
    return lax.dot_general(a, b, (((ca,), (cb,)), ((), ())), preferred_element_type=F32)


def feature(values):
    return jnp.where(values > 0, values + 1.0, jnp.exp(jnp.minimum(values, 0.0)))


def feature_slope(values):
    return jnp.where(values > 0, 1.0, jnp.exp(jnp.minimum(values, 0.0)))


def body(
    tok_in, cot_in, wq_in, wk_in, rate_in, reset_in,
    out, igrad, gq, gk,
    tok, cot, wq, wk, rate, reset, tokt, w, rt, sin, rin, zt, zs, zm, za, zb, sb, read, feat, slope, bg,
    gown, gsnd, grcv, hb, r1, fin, r3,
    s_l, s_zs, s_zr, s_y, s_w, s_rx, s_rz, s_in, s_a, s_bs, s_br, s_bk, s_c, s_xy, s_e,
):
    rows, width = tok.shape
    shard = wq.shape[1]
    wide = width // (CHUNKS * X)
    block_width = min(wide, C * shard)
    nz = ZL * ZH
    reach = (ZH - 1) * ZL // 2
    s = lax.axis_index("seg")
    b = lax.axis_index("dp")
    zl, x = s // X, s % X
    y, zh, c = b // (ZH * C), (b // C) % ZH, b % C
    zi = zh * ZL + zl

    def dev(zl=zl, x=x, y=y, zh=zh, c=c):
        return (zl * X + x, (y * ZH + zh) * C + c)

    started = []

    def make(src, dst, send_sem, recv_sem, target):
        return pltpu.make_async_remote_copy(
            src_ref=src, dst_ref=dst, send_sem=send_sem, recv_sem=recv_sem,
            device_id=target, device_id_type=MESH,
        )

    def send(src, dst, sem, at, target):
        copy = make(src, dst, sem.at[(0,) + at], sem.at[(1,) + at], target)
        copy.start()
        started.append(copy)
        return copy

    moves = ((wk_in, wk), (wq_in, wq), (rate_in, rate), (reset_in, reset), (tok_in, tok), (cot_in, cot))
    loads = [pltpu.make_async_copy(src, dst, s_l.at[i]) for i, (src, dst) in enumerate(moves)]
    for copy in loads:
        copy.start()
    za[...] = jnp.zeros_like(za)
    zb[...] = jnp.zeros_like(zb)
    peers = [dev(c=1 - c)]
    peers += [dev(x=(x + k) % X) for k in range(1, X)]
    peers += [dev(y=(y + k) % Y) for k in range(1, Y)]
    peers += [dev(zl=(zl + k) % ZL) for k in range(1, ZL)]
    near = len(peers)
    for o in range(1, ZH):
        peers.append(dev(zl=jnp.where(o * ZL - zl <= reach, 0, ZL - 1), zh=(zh + o) % ZH))
    edge = (zl == 0) | (zl == ZL - 1)
    barrier = pltpu.get_barrier_semaphore()
    for peer in peers[::-1]:
        pl.semaphore_signal(barrier, inc=1, device_id=peer, device_id_type=MESH)
    for copy in loads[:4]:
        copy.wait()
    lanes = pl.ds(pl.multiple_of(c * shard, shard), shard)
    w[QUERY, y, zh, :, lanes] = wq[...]
    w[WRITE, y, zh, :, lanes] = wk[...]
    factor = jnp.exp(-rate[...]) * (1 - reset[...]).astype(F32)
    factor = jnp.concatenate([factor, jnp.zeros_like(factor)], axis=1)
    rt[zl, x] = jnp.broadcast_to(factor, rt.shape[2:])
    pl.semaphore_wait(barrier, near + jnp.where(edge, reach, 0))

    def block(part, o):
        return w.at[part, y, (zh + o) % ZH, :, lanes]

    spread = []
    for part in (WRITE, QUERY):
        for d in range(reach, 0, -1):
            zt_ = (zi + jnp.where(zl == 0, -d, d) + nz) % nz
            o = (d - 1) // ZL + 1
            o = jnp.where(zl == 0, o, ZH - o)
            spread.append(make(
                block(part, 0), block(part, 0), s_zs.at[part, d], s_zr.at[part, o],
                dev(zl=zt_ % ZL, zh=zt_ // ZL),
            ))

    @pl.when(edge)
    def _():
        for copy in spread:
            copy.start()

    def arrive_z(part, o):
        make(block(part, o), block(part, o), s_zs.at[part, 0], s_zr.at[part, o], dev(zh=(zh + 1) % ZH)).wait_recv()

    along_y = {}

    def start_y(part, o):
        along_y[part, o] = [
            send(block(part, o), block(part, o), s_y, (part, o, k), dev(y=(y + k) % Y)) for k in range(1, Y)
        ]

    to_core = {WRITE: []}

    def start_core(part, o):
        for copy in along_y[part, o]:
            copy.wait_recv()
        column = w.at[part, :, (zh + o) % ZH, :, lanes]
        to_core[part].append(send(column, column, s_w, (part, o), dev(c=1 - c)))

    def left():
        for copy in started:
            copy.wait_send()
        started.clear()

    def left_early():
        left()

        @pl.when(edge)
        def _():
            for copy in spread:
                copy.wait_send()

        for way, j in plan:
            @pl.when(place[way] % 2 == 0)
            def _():
                pass_a(way, j).wait_send()

            @pl.when(place[way] == 1)
            def _():
                pass_b(way, j, 1).wait_send()
                pass_b(way, j, 2).wait_send()

    offsets = sorted(range(1, ZH), key=lambda o: min(o, ZH - o))
    start_y(WRITE, 0)
    own = rt.at[zl, x]
    gotx = [send(own, own, s_rx, (k,), dev(x=(x + k) % X)) for k in range(1, X)]
    loads[4].wait()
    step = width // 8
    for n in range(8):
        tokt[n * step:(n + 1) * step] = tok[:, n * step:(n + 1) * step].T
    for copy in gotx:
        copy.wait_recv()
    own = rt.at[zl]
    gotz = [send(own, own, s_rz, (k,), dev(zl=(zl + k) % ZL)) for k in range(1, ZL)]
    loads[5].wait()
    for o in offsets:
        arrive_z(WRITE, o)
        start_y(WRITE, o)
    for o in [0] + offsets:
        start_core(WRITE, o)
    for o in offsets:
        arrive_z(QUERY, o)
    line = w.at[QUERY, y, :, :, lanes]
    queries_y = [send(line, line, s_y, (QUERY, 0, k), dev(y=(y + k) % Y)) for k in range(1, Y)]
    for copy in to_core[WRITE]:
        copy.wait_recv()

    pairs = [(n // ZH, n % ZH, slice(n * C * shard, (n + 1) * C * shard)) for n in range(Y * ZH)]

    def turned(part):
        total = jnp.zeros((KEY, rows), F32)
        for i, j, at in pairs:
            total = total + dot(w[part, i, j], tok[:, at], 1, 1)
        return feature(total).astype(BF16)

    def straight(part):
        total = jnp.zeros((rows, KEY), F32)
        for i, j, at in pairs:
            total = total + dot(tok[:, at], w[part, i, j], 1, 1)
        feat[part] = feature(total).astype(BF16)
        slope[part] = feature_slope(total)

    ins = {}

    def exchange(way, weights, values, scale):
        for j in range(CHUNKS):
            at = slice(j * X * wide, (j + 1) * X * wide)
            term = (dot(weights, values[:, at], 1, 0) * scale).astype(BF16)
            for q in range(X):
                sin[way, j, q] = term[:, q * wide:(q + 1) * wide]
            ins[way, j] = [
                send(sin.at[way, j, (x + k) % X], rin.at[way, j, x], s_in, (way, j, k), dev(x=(x + k) % X))
                for k in range(1, X)
            ]
            rin[way, j, x] = sin[way, j, x]

    exchange(FORE, turned(WRITE), tok, 1.0 / rows)
    straight(WRITE)
    for copy in queries_y:
        copy.wait_recv()
    column = w.at[QUERY, :, :, :, lanes]
    send(column, column, s_w, (QUERY, 0), dev(c=1 - c)).wait_recv()
    exchange(BACK, turned(QUERY), cot, 1.0)
    straight(QUERY)

    eye = lax.broadcasted_iota(jnp.int32, (KEY, KEY), 0) == lax.broadcasted_iota(jnp.int32, (KEY, KEY), 1)

    def column(row):
        return jnp.sum(jnp.where(eye, row[0:1, :KEY], 0.0), axis=1, keepdims=True)

    for copy in gotz:
        copy.wait_recv()
    keep = [column(rt[zl, i]) for i in range(X)]
    whole = keep[0]
    for i in range(1, X):
        whole = whole * keep[i]
    place = {FORE: zl, BACK: ZL - 1 - zl}
    ahead = {FORE: 1, BACK: -1}
    order = {FORE: list(range(X)), BACK: list(range(X))[::-1]}
    from_a, from_b = {}, {}
    for way, row in ((FORE, ZL - 2), (BACK, 1)):
        skipped = column(rt[row, 0])
        for i in range(1, X):
            skipped = skipped * column(rt[row, i])
        one = jnp.ones_like(skipped)
        p = place[way]
        from_a[way] = jnp.where(p % 2 == 1, one, 0.0)
        from_b[way] = jnp.where(p == 2, one, jnp.where(p == 3, skipped, 0.0))

    later = []

    def hop(way, steps):
        return dev(zl=(zl + ahead[way] * steps + ZL) % ZL)

    def pass_a(way, j):
        return make(zs.at[way, j], za.at[way, j], s_a.at[0, way, j], s_a.at[1, way, j], hop(way, 1))

    def pass_b(way, j, n):
        return make(zm.at[way, j], zb.at[way, j], s_bs.at[way, j, n], s_br.at[way, j], hop(way, n))

    def totals(way, j):
        for copy in ins[way, j]:
            copy.wait_recv()
        total = rin[way, j, order[way][0]].astype(F32)
        for i in order[way][1:]:
            total = keep[i] * total + rin[way, j, i].astype(F32)
        zt[way, j] = total
        zs[way, j] = total.astype(BF16)

        @pl.when(place[way] % 2 == 0)
        def _():
            pass_a(way, j).start()

    def relay(way, j):
        @pl.when(place[way] == 1)
        def _():
            pass_a(way, j).wait_recv()
            zm[way, j] = (whole * za[way, j].astype(F32) + zt[way, j]).astype(BF16)
            pass_b(way, j, 1).start()
            pass_b(way, j, 2).start()

    backs = {}

    def finish(way, j):
        @pl.when(place[way] >= 2)
        def _():
            pass_b(way, j, 1).wait_recv()

        @pl.when(place[way] == 3)
        def _():
            pass_a(way, j).wait_recv()

        state = from_a[way] * za[way, j].astype(F32) + from_b[way] * zb[way, j].astype(F32)
        for n, i in enumerate(order[way]):
            sb[way, j, i] = state.astype(BF16)
            if n < X - 1:
                state = keep[i] * state + rin[way, j, i].astype(F32)
        backs[way, j] = [
            send(sb.at[way, j, (x + k) % X], read.at[way, j, x], s_bk, (way, j, k), dev(x=(x + k) % X))
            for k in range(1, X)
        ]
        read[way, j, x] = sb[way, j, x]

    plan = [(way, j) for way in (FORE, BACK) for j in range(CHUNKS)]
    for n in range(len(plan) + 2):
        if n < len(plan):
            totals(*plan[n])
        if 1 <= n <= len(plan):
            relay(*plan[n - 1])
        if n >= 2:
            finish(*plan[n - 2])

    half = ZL // 2
    span = width // ZL
    per = span // (X * Y * ZH * C)
    blank = jnp.zeros((rows, KEY), BF16)
    pair, plane = {}, {}

    def against(way, values, js):
        total = jnp.zeros((rows, KEY), F32)
        for j in js:
            for copy in backs[way, j]:
                copy.wait_recv()
            for q in range(X):
                at = slice((j * X + q) * wide, (j * X + q + 1) * wide)
                total = total + dot(values[:, at], read[way, j, q], 1, 1)
        return total

    def product(part, grad):
        low = jnp.concatenate([grad, blank], axis=1)
        high = jnp.concatenate([blank, grad], axis=1)
        for z in range(half):
            g = dot(tokt[z * span:(z + 1) * span], low, 1, 0)
            g = g + dot(tokt[(z + half) * span:(z + half + 1) * span], high, 1, 0)
            g = g.reshape(X * Y * ZH, C, per, 2 * KEY)
            first = g[:, 0].reshape(X, Y, ZH * per, 2 * KEY)
            second = g[:, 1].reshape(X, Y, ZH * per, 2 * KEY)
            gown[part, z] = jnp.where(c == 0, first, second)
            gsnd[part, z] = jnp.where(c == 0, second, first).astype(BF16)
            pair[part, z] = send(gsnd.at[part, z], grcv.at[part, z], s_c, (part, z), dev(c=1 - c))

    def over_plane(part):
        for z in range(half):
            pair[part, z].wait_recv()
            total = gown[part, z] + grcv[part, z].astype(F32)
            gown[part, z] = total
            hb[part, z] = total.astype(BF16)
        plane[part] = []
        for k in sorted(range(1, X * Y), key=lambda k: -min(k // Y, X - k // Y) - min(k % Y, Y - k % Y)):
            xt, yt = (x + k // Y) % X, (y + k % Y) % Y
            plane[part].append(send(hb.at[part, :, xt, yt], r1.at[part, k], s_xy, (part, k), dev(x=xt, y=yt)))

    def gather_plane(part):
        for copy in plane[part]:
            copy.wait_recv()
        total = gown[part, :, x, y]
        for k in range(1, X * Y):
            total = total + r1[part, k].astype(F32)
        for h in range(2):
            piece = total[:, :, h * KEY:(h + 1) * KEY].reshape(half, ZH, per, KEY)
            fin[h * half:(h + 1) * half, :, :, part * KEY:(part + 1) * KEY] = piece

    query_grad = (against(FORE, cot, range(CHUNKS)) * slope[QUERY]).astype(BF16)
    bg[QUERY] = query_grad
    product(QUERY, query_grad)
    wanted = against(BACK, tok, range(CHUNKS - 1))
    over_plane(QUERY)
    wanted = wanted + against(BACK, tok, range(CHUNKS - 1, CHUNKS))
    key_grad = (wanted / rows * slope[WRITE]).astype(BF16)
    bg[WRITE] = key_grad
    product(WRITE, key_grad)
    over_plane(WRITE)

    for j in range(CHUNKS):
        for q in range(X):
            at = slice((j * X + q) * wide, (j * X + q + 1) * wide)
            out[:, at] = (tok[:, at].astype(F32) + dot(feat[QUERY], read[FORE, j, q], 1, 0)).astype(BF16)
    early = started[:]
    started[:] = [copy for copy in early if not any(copy is other for part in plane for other in plane[part])]
    kept = [copy for copy in early if not any(copy is other for other in started)]
    left_early()
    gather_plane(QUERY)
    gather_plane(WRITE)
    last = []
    for k in sorted(range(1, nz), key=lambda k: -min(k, nz - k)):
        zt_ = (zi + k) % nz
        last.append(send(fin.at[zt_ % ZL, zt_ // ZL], r3.at[k], s_e, (k,), dev(zl=zt_ % ZL, zh=zt_ // ZL)))

    for n in range(0, width, block_width):
        at = slice(n, n + block_width)
        j, q, k = n // (X * wide), n // wide % X, n % wide
        i, m, n = n // (ZH * C * shard), n // (C * shard) % ZH, n % (C * shard)
        total = cot[:, at].astype(F32) + dot(feat[WRITE], read[BACK, j, q, :, k:k + block_width], 1, 0) / rows
        for part in (QUERY, WRITE):
            total = total + dot(bg[part], w[part, i, m, :, n:n + block_width], 1, 0)
        igrad[:, at] = total.astype(BF16)
    for copy in kept:
        copy.wait_send()
    for copy in last:
        copy.wait_recv()
    total = fin[zl, zh]
    for k in range(1, nz):
        total = total + r3[k]
    gq[...] = total[:, :KEY]
    gk[...] = total[:, KEY:]

    left()


def publish(*refs):
    copies = [pltpu.make_async_copy(refs[i], refs[4 + i], refs[8].at[i]) for i in range(4)]
    for copy in copies:
        copy.start()
    for copy in copies:
        copy.wait()


def local(tokens, cotangent, query_weight, key_weight, forget_rate, resets):
    rows, width = tokens.shape[2:]
    shard = query_weight.shape[0]
    wide = width // (CHUNKS * X)
    half = ZL // 2
    span = width // ZL
    per = span // (X * Y * ZH * C)
    nz = ZL * ZH
    reach = (ZH - 1) * ZL // 2
    lanes = 2 * KEY
    vm = pltpu.VMEM
    sem = pltpu.SemaphoreType.DMA
    scratch = [
        vm((rows, width), BF16),
        vm((rows, width), BF16),
        vm((KEY, shard), BF16),
        vm((KEY, shard), BF16),
        vm((1, KEY), F32),
        vm((1, 1), jnp.int32),
        vm((width, rows), BF16),
        vm((2, Y, ZH, KEY, C * shard), BF16),
        vm((ZL, X, 8, lanes), F32),
        vm((2, CHUNKS, X, KEY, wide), BF16),
        vm((2, CHUNKS, X, KEY, wide), BF16),
        vm((2, CHUNKS, KEY, wide), F32),
        vm((2, CHUNKS, KEY, wide), BF16),
        vm((2, CHUNKS, KEY, wide), BF16),
        vm((2, CHUNKS, KEY, wide), BF16),
        vm((2, CHUNKS, KEY, wide), BF16),
        vm((2, CHUNKS, X, KEY, wide), BF16),
        vm((2, CHUNKS, X, KEY, wide), BF16),
        vm((2, rows, KEY), BF16),
        vm((2, rows, KEY), F32),
        vm((2, rows, KEY), BF16),
        vm((2, half, X, Y, ZH * per, lanes), F32),
        vm((2, half, X, Y, ZH * per, lanes), BF16),
        vm((2, half, X, Y, ZH * per, lanes), BF16),
        vm((2, half, X, Y, ZH * per, lanes), BF16),
        vm((2, X * Y, half, ZH * per, lanes), BF16),
        vm((ZL, ZH, per, lanes), F32),
        vm((nz, per, lanes), F32),
        sem((6,)), sem((2, reach + 1)), sem((2, ZH)), sem((2, 2, ZH, Y)), sem((2, 2, ZH)),
        sem((2, X)), sem((2, ZL)), sem((2, 2, CHUNKS, X)), sem((2, 2, CHUNKS)),
        sem((2, CHUNKS, 3)), sem((2, CHUNKS)), sem((2, 2, CHUNKS, X)), sem((2, 2, half)),
        sem((2, 2, X * Y)), sem((2, nz)),
    ]
    anywhere = pl.BlockSpec(memory_space=pl.ANY)
    whole = pl.BlockSpec(memory_space=pltpu.VMEM)
    shapes = (
        jax.ShapeDtypeStruct((rows, width), BF16),
        jax.ShapeDtypeStruct((rows, width), BF16),
        jax.ShapeDtypeStruct((per, KEY), F32),
        jax.ShapeDtypeStruct((per, KEY), F32),
    )
    results = pl.pallas_call(
        body,
        out_shape=tuple(vm(r.shape, r.dtype) for r in shapes),
        in_specs=[anywhere] * 6,
        out_specs=(whole,) * 4,
        scratch_shapes=scratch,
        compiler_params=pltpu.CompilerParams(
            collective_id=0, has_side_effects=True, vmem_limit_bytes=VMEM_LIMIT
        ),
        cost_estimate=pl.CostEstimate(
            flops=16 * rows * width * KEY, bytes_accessed=8 * rows * width, transcendentals=rows * lanes
        ),
    )(tokens[0, 0], cotangent[0, 0], query_weight.T, key_weight.T, forget_rate[0], resets)
    output, input_grad, grad_query, grad_key = pl.pallas_call(
        publish,
        out_shape=shapes,
        in_specs=[anywhere] * 4,
        out_specs=(anywhere,) * 4,
        scratch_shapes=[sem((4,))], compiler_params=pltpu.CompilerParams(vmem_limit_bytes=16 * 1024 * 1024),
    )(*results)
    return output[None, None], input_grad[None, None], grad_query, grad_key


def solution(mesh):
    placed = (
        P("seg", "dp", None, None),
        P("seg", "dp", None, None),
        P("dp", None),
        P("dp", None),
        P("seg", "dp", None),
        P("seg", "dp"),
    )
    return jax.shard_map(
        local,
        mesh=mesh,
        in_specs=placed,
        out_specs=(
            P("seg", "dp", None, None),
            P("seg", "dp", None, None),
            P(("seg", "dp"), None),
            P(("seg", "dp"), None),
        ),
        check_vma=False,
    )
```

```python
import jax
import jax.numpy as jnp
from jax import lax
from jax.experimental import pallas as pl
from jax.experimental.pallas import tpu as pltpu
from jax.sharding import PartitionSpec as P

ZL, X = 4, 4
Y, ZH, C = 4, 4, 2
CHUNKS = 2
KEY = 64
VMEM_LIMIT = 56 * 1024 * 1024
F32 = jnp.float32
BF16 = jnp.bfloat16
MESH = pl.DeviceIdType.MESH
QUERY, WRITE = 0, 1
FORE, BACK = 0, 1


def dot(a, b, ca, cb):
    return lax.dot_general(a, b, (((ca,), (cb,)), ((), ())), preferred_element_type=F32)


def feature(values):
    return jnp.where(values > 0, values + 1.0, jnp.exp(jnp.minimum(values, 0.0)))


def feature_slope(values):
    return jnp.where(values > 0, 1.0, jnp.exp(jnp.minimum(values, 0.0)))


def body(
    tok_in, cot_in, wq_in, wk_in, rate_in, reset_in,
    out, igrad, gq, gk,
    tok, cot, wq, wk, rate, reset, tt, tsend, w, rt, sin, rin, zt, zs, zm, za, zb, sb, read, feat, slope, bg, bgs,
    gown, hb, r1, fin, r3,
    s_l, s_zs, s_zr, s_y, s_w, s_rx, s_rz, s_in, s_a, s_bs, s_br, s_bk, s_c, s_t, s_xy, s_e,
):
    rows, width = tok.shape
    shard = wq.shape[1]
    wide = width // (CHUNKS * X)
    span = width // (ZL * C)
    per = span // (X * Y * ZH)
    block_width = min(wide, C * shard)
    nz = ZL * ZH
    reach = (ZH - 1) * ZL // 2
    s = lax.axis_index("seg")
    b = lax.axis_index("dp")
    zl, x = s // X, s % X
    y, zh, c = b // (ZH * C), (b // C) % ZH, b % C
    zi = zh * ZL + zl

    def dev(zl=zl, x=x, y=y, zh=zh, c=c):
        return (zl * X + x, (y * ZH + zh) * C + c)

    started = []

    def make(src, dst, send_sem, recv_sem, target):
        return pltpu.make_async_remote_copy(
            src_ref=src, dst_ref=dst, send_sem=send_sem, recv_sem=recv_sem,
            device_id=target, device_id_type=MESH,
        )

    def send(src, dst, sem, at, target):
        copy = make(src, dst, sem.at[(0,) + at], sem.at[(1,) + at], target)
        copy.start()
        started.append(copy)
        return copy

    moves = ((wk_in, wk), (wq_in, wq), (rate_in, rate), (reset_in, reset), (tok_in, tok), (cot_in, cot))
    loads = [pltpu.make_async_copy(src, dst, s_l.at[i]) for i, (src, dst) in enumerate(moves)]
    for copy in loads:
        copy.start()
    za[...] = jnp.zeros_like(za)
    zb[...] = jnp.zeros_like(zb)
    peers = [dev(c=1 - c)]
    peers += [dev(x=(x + k) % X) for k in range(1, X)]
    peers += [dev(y=(y + k) % Y) for k in range(1, Y)]
    peers += [dev(zl=(zl + k) % ZL) for k in range(1, ZL)]
    near = len(peers)
    for o in range(1, ZH):
        peers.append(dev(zl=jnp.where(o * ZL - zl <= reach, 0, ZL - 1), zh=(zh + o) % ZH))
    edge = (zl == 0) | (zl == ZL - 1)
    barrier = pltpu.get_barrier_semaphore()
    for peer in peers[::-1]:
        pl.semaphore_signal(barrier, inc=1, device_id=peer, device_id_type=MESH)
    for copy in loads[:4]:
        copy.wait()
    lanes = pl.ds(pl.multiple_of(c * shard, shard), shard)
    w[QUERY, y, zh, :, lanes] = wq[...]
    w[WRITE, y, zh, :, lanes] = wk[...]
    factor = jnp.exp(-rate[...]) * (1 - reset[...]).astype(F32)
    factor = jnp.concatenate([factor, jnp.zeros_like(factor)], axis=1)
    rt[zl, x] = jnp.broadcast_to(factor, rt.shape[2:])
    pl.semaphore_wait(barrier, near + jnp.where(edge, reach, 0))

    def block(part, o):
        return w.at[part, y, (zh + o) % ZH, :, lanes]

    spread = []
    for part in (WRITE, QUERY):
        for d in range(reach, 0, -1):
            zt_ = (zi + jnp.where(zl == 0, -d, d) + nz) % nz
            o = (d - 1) // ZL + 1
            o = jnp.where(zl == 0, o, ZH - o)
            spread.append(make(
                block(part, 0), block(part, 0), s_zs.at[part, d], s_zr.at[part, o],
                dev(zl=zt_ % ZL, zh=zt_ // ZL),
            ))

    @pl.when(edge)
    def _():
        for copy in spread:
            copy.start()

    def arrive_z(part, o):
        make(block(part, o), block(part, o), s_zs.at[part, 0], s_zr.at[part, o], dev(zh=(zh + 1) % ZH)).wait_recv()

    along_y = {}

    def start_y(part, o):
        along_y[part, o] = [
            send(block(part, o), block(part, o), s_y, (part, o, k), dev(y=(y + k) % Y))
            for k in sorted(range(1, Y), key=lambda k: -min(k, Y - k))
        ]

    to_core = {WRITE: []}

    def start_core(part, o):
        for copy in along_y[part, o]:
            copy.wait_recv()
        column = w.at[part, :, (zh + o) % ZH, :, lanes]
        to_core[part].append(send(column, column, s_w, (part, o), dev(c=1 - c)))

    def left():
        for copy in started:
            copy.wait_send()
        started.clear()

    def left_early():
        left()

        @pl.when(edge)
        def _():
            for copy in spread:
                copy.wait_send()

        for way, j in plan:
            @pl.when(place[way] % 2 == 0)
            def _():
                pass_a(way, j).wait_send()

            @pl.when(place[way] == 1)
            def _():
                pass_b(way, j, 1).wait_send()
                pass_b(way, j, 2).wait_send()

    offsets = sorted(range(1, ZH), key=lambda o: min(o, ZH - o))
    start_y(WRITE, 0)
    own = rt.at[zl, x]
    gotx = [send(own, own, s_rx, (k,), dev(x=(x + k) % X)) for k in range(1, X)]
    loads[4].wait()
    step = width // 8
    for n in range(8):
        piece = tok[:, n * step:(n + 1) * step].astype(F32).T.reshape(step // (C * per), C, per, rows)
        first = piece[:, 0].reshape(step // C, rows)
        second = piece[:, 1].reshape(step // C, rows)
        at = slice(n * step // C, (n + 1) * step // C)
        tt[at, :rows] = jnp.where(c == 0, first, second).astype(BF16)
        tsend[at] = jnp.where(c == 0, second, first).astype(BF16)
    got_tokens = send(tsend, tt.at[:, pl.ds(rows, rows)], s_t, (), dev(c=1 - c))
    for copy in gotx:
        copy.wait_recv()
    own = rt.at[zl]
    gotz = [send(own, own, s_rz, (k,), dev(zl=(zl + k) % ZL)) for k in range(1, ZL)]
    loads[5].wait()
    for o in offsets:
        arrive_z(WRITE, o)
        start_y(WRITE, o)
    for o in [0] + offsets:
        start_core(WRITE, o)
    for o in offsets:
        arrive_z(QUERY, o)
    line = w.at[QUERY, y, :, :, lanes]
    queries_y = [send(line, line, s_y, (QUERY, 0, k), dev(y=(y + k) % Y)) for k in range(1, Y)]
    for copy in to_core[WRITE]:
        copy.wait_recv()

    pairs = [(n // ZH, n % ZH, slice(n * C * shard, (n + 1) * C * shard)) for n in range(Y * ZH)]

    def turned(part):
        total = jnp.zeros((KEY, rows), F32)
        for i, j, at in pairs:
            total = total + dot(w[part, i, j], tok[:, at], 1, 1)
        return feature(total).astype(BF16)

    def straight(part):
        total = jnp.zeros((rows, KEY), F32)
        for i, j, at in pairs:
            total = total + dot(tok[:, at], w[part, i, j], 1, 1)
        feat[part] = feature(total).astype(BF16)
        slope[part] = feature_slope(total)

    ins = {}

    def exchange(way, weights, values, scale):
        for j in range(CHUNKS):
            at = slice(j * X * wide, (j + 1) * X * wide)
            term = (dot(weights, values[:, at], 1, 0) * scale).astype(BF16)
            for q in range(X):
                sin[way, j, q] = term[:, q * wide:(q + 1) * wide]
            ins[way, j] = [
                send(sin.at[way, j, (x + k) % X], rin.at[way, j, x], s_in, (way, j, k), dev(x=(x + k) % X))
                for k in sorted(range(1, X), key=lambda k: -min(k, X - k))
            ]
            rin[way, j, x] = sin[way, j, x]

    exchange(FORE, turned(WRITE), tok, 1.0 / rows)
    straight(WRITE)

    eye = lax.broadcasted_iota(jnp.int32, (KEY, KEY), 0) == lax.broadcasted_iota(jnp.int32, (KEY, KEY), 1)

    def column(row):
        return jnp.sum(jnp.where(eye, row[0:1, :KEY], 0.0), axis=1, keepdims=True)

    for copy in gotz:
        copy.wait_recv()
    keep = [column(rt[zl, i]) for i in range(X)]
    whole = keep[0]
    for i in range(1, X):
        whole = whole * keep[i]
    place = {FORE: zl, BACK: ZL - 1 - zl}
    ahead = {FORE: 1, BACK: -1}
    order = {FORE: list(range(X)), BACK: list(range(X))[::-1]}
    from_a, from_b = {}, {}
    for way, row in ((FORE, ZL - 2), (BACK, 1)):
        skipped = column(rt[row, 0])
        for i in range(1, X):
            skipped = skipped * column(rt[row, i])
        one = jnp.ones_like(skipped)
        p = place[way]
        from_a[way] = jnp.where(p % 2 == 1, one, 0.0)
        from_b[way] = jnp.where(p == 2, one, jnp.where(p == 3, skipped, 0.0))

    for copy in queries_y:
        copy.wait_recv()
    column = w.at[QUERY, :, :, :, lanes]
    send(column, column, s_w, (QUERY, 0), dev(c=1 - c)).wait_recv()
    exchange(BACK, turned(QUERY), cot, 1.0)


    def hop(way, steps):
        return dev(zl=(zl + ahead[way] * steps + ZL) % ZL)

    def pass_a(way, j):
        return make(zs.at[way, j], za.at[way, j], s_a.at[0, way, j], s_a.at[1, way, j], hop(way, 1))

    def pass_b(way, j, n):
        return make(zm.at[way, j], zb.at[way, j], s_bs.at[way, j, n], s_br.at[way, j], hop(way, n))

    def totals(way, j):
        for copy in ins[way, j]:
            copy.wait_recv()
        total = rin[way, j, order[way][0]].astype(F32)
        for i in order[way][1:]:
            total = keep[i] * total + rin[way, j, i].astype(F32)
        zt[way, j] = total
        zs[way, j] = total.astype(BF16)

        @pl.when(place[way] % 2 == 0)
        def _():
            pass_a(way, j).start()

    def relay(way, j):
        @pl.when(place[way] == 1)
        def _():
            pass_a(way, j).wait_recv()
            zm[way, j] = (whole * za[way, j].astype(F32) + zt[way, j]).astype(BF16)
            pass_b(way, j, 1).start()
            pass_b(way, j, 2).start()

    backs = {}

    def finish(way, j):
        @pl.when(place[way] >= 2)
        def _():
            pass_b(way, j, 1).wait_recv()

        @pl.when(place[way] == 3)
        def _():
            pass_a(way, j).wait_recv()

        state = from_a[way] * za[way, j].astype(F32) + from_b[way] * zb[way, j].astype(F32)
        for n, i in enumerate(order[way]):
            sb[way, j, i] = state.astype(BF16)
            if n < X - 1:
                state = keep[i] * state + rin[way, j, i].astype(F32)
        backs[way, j] = [
            send(sb.at[way, j, (x + k) % X], read.at[way, j, x], s_bk, (way, j, k), dev(x=(x + k) % X))
            for k in sorted(range(1, X), key=lambda k: -min(k, X - k))
        ]
        read[way, j, x] = sb[way, j, x]

    plan = [(way, j) for way in (FORE, BACK) for j in range(CHUNKS)]
    for n in range(len(plan) + 2):
        if n < len(plan):
            totals(*plan[n])
        if 1 <= n <= len(plan):
            relay(*plan[n - 1])
        if n >= 2:
            finish(*plan[n - 2])
    straight(QUERY)

    half = ZL // 2
    blank = jnp.zeros((C * rows, KEY), BF16)
    other, plane = {}, {}
    got_tokens.wait_recv()

    def against(way, values, js):
        total = jnp.zeros((rows, KEY), F32)
        for j in js:
            for copy in backs[way, j]:
                copy.wait_recv()
            for q in range(X):
                at = slice((j * X + q) * wide, (j * X + q + 1) * wide)
                total = total + dot(values[:, at], read[way, j, q], 1, 1)
        return total

    def share(part, grad):
        bg[part] = grad
        other[part] = send(bg.at[part], bgs.at[part], s_c, (part,), dev(c=1 - c))

    def over_plane(part):
        other[part].wait_recv()
        grads = jnp.concatenate([bg[part], bgs[part]], axis=0)
        low = jnp.concatenate([grads, blank], axis=1)
        high = jnp.concatenate([blank, grads], axis=1)
        for z in range(half):
            g = dot(tt[z * span:(z + 1) * span], low, 1, 0)
            g = g + dot(tt[(z + half) * span:(z + half + 1) * span], high, 1, 0)
            g = g.reshape(X, Y, ZH * per, 2 * KEY)
            gown[part, z] = g
            hb[part, z] = g.astype(BF16)
        plane[part] = []
        for k in sorted(range(1, X * Y), key=lambda k: -min(k // Y, X - k // Y) - min(k % Y, Y - k % Y)):
            xt, yt = (x + k // Y) % X, (y + k % Y) % Y
            plane[part].append(send(hb.at[part, :, xt, yt], r1.at[part, k], s_xy, (part, k), dev(x=xt, y=yt)))

    def gather_plane(part):
        for copy in plane[part]:
            copy.wait_recv()
        total = gown[part, :, x, y]
        for k in range(1, X * Y):
            total = total + r1[part, k].astype(F32)
        for h in range(2):
            piece = total[:, :, h * KEY:(h + 1) * KEY].reshape(half, ZH, per, KEY)
            fin[h * half:(h + 1) * half, :, :, part * KEY:(part + 1) * KEY] = piece

    query_grad = (against(FORE, cot, range(CHUNKS)) * slope[QUERY]).astype(BF16)
    share(QUERY, query_grad)
    wanted = against(BACK, tok, range(CHUNKS - 1))
    over_plane(QUERY)
    wanted = wanted + against(BACK, tok, range(CHUNKS - 1, CHUNKS))
    key_grad = (wanted / rows * slope[WRITE]).astype(BF16)
    share(WRITE, key_grad)
    over_plane(WRITE)

    for j in range(CHUNKS):
        for q in range(X):
            at = slice((j * X + q) * wide, (j * X + q + 1) * wide)
            out[:, at] = (tok[:, at].astype(F32) + dot(feat[QUERY], read[FORE, j, q], 1, 0)).astype(BF16)
    early = started[:]
    started[:] = [copy for copy in early if not any(copy is other for part in plane for other in plane[part])]
    kept = [copy for copy in early if not any(copy is other for other in started)]
    left_early()
    gather_plane(QUERY)
    gather_plane(WRITE)
    last = []
    for k in sorted(range(1, nz), key=lambda k: -min(k, nz - k)):
        zt_ = (zi + k) % nz
        last.append(send(fin.at[zt_ % ZL, zt_ // ZL], r3.at[k], s_e, (k,), dev(zl=zt_ % ZL, zh=zt_ // ZL)))

    for n in range(0, width, block_width):
        at = slice(n, n + block_width)
        j, q, k = n // (X * wide), n // wide % X, n % wide
        i, m, n = n // (ZH * C * shard), n // (C * shard) % ZH, n % (C * shard)
        total = cot[:, at].astype(F32) + dot(feat[WRITE], read[BACK, j, q, :, k:k + block_width], 1, 0) / rows
        for part in (QUERY, WRITE):
            total = total + dot(bg[part], w[part, i, m, :, n:n + block_width], 1, 0)
        igrad[:, at] = total.astype(BF16)
    for copy in kept:
        copy.wait_send()
    for copy in last:
        copy.wait_recv()
    total = fin[zl, zh]
    for k in range(1, nz):
        total = total + r3[k]
    gq[...] = total[:, :KEY]
    gk[...] = total[:, KEY:]

    left()


def publish(*refs):
    copies = [pltpu.make_async_copy(refs[i], refs[4 + i], refs[8].at[i]) for i in range(4)]
    for copy in copies:
        copy.start()
    for copy in copies:
        copy.wait()


def local(tokens, cotangent, query_weight, key_weight, forget_rate, resets):
    rows, width = tokens.shape[2:]
    shard = query_weight.shape[0]
    wide = width // (CHUNKS * X)
    half = ZL // 2
    span = width // ZL
    per = span // (X * Y * ZH * C)
    nz = ZL * ZH
    reach = (ZH - 1) * ZL // 2
    lanes = 2 * KEY
    vm = pltpu.VMEM
    sem = pltpu.SemaphoreType.DMA
    scratch = [
        vm((rows, width), BF16),
        vm((rows, width), BF16),
        vm((KEY, shard), BF16),
        vm((KEY, shard), BF16),
        vm((1, KEY), F32),
        vm((1, 1), jnp.int32),
        vm((width // C, C * rows), BF16),
        vm((width // C, rows), BF16),
        vm((2, Y, ZH, KEY, C * shard), BF16),
        vm((ZL, X, 8, lanes), F32),
        vm((2, CHUNKS, X, KEY, wide), BF16),
        vm((2, CHUNKS, X, KEY, wide), BF16),
        vm((2, CHUNKS, KEY, wide), F32),
        vm((2, CHUNKS, KEY, wide), BF16),
        vm((2, CHUNKS, KEY, wide), BF16),
        vm((2, CHUNKS, KEY, wide), BF16),
        vm((2, CHUNKS, KEY, wide), BF16),
        vm((2, CHUNKS, X, KEY, wide), BF16),
        vm((2, CHUNKS, X, KEY, wide), BF16),
        vm((2, rows, KEY), BF16),
        vm((2, rows, KEY), F32),
        vm((2, rows, KEY), BF16),
        vm((2, rows, KEY), BF16),
        vm((2, half, X, Y, ZH * per, lanes), F32),
        vm((2, half, X, Y, ZH * per, lanes), BF16),
        vm((2, X * Y, half, ZH * per, lanes), BF16),
        vm((ZL, ZH, per, lanes), F32),
        vm((nz, per, lanes), F32),
        sem((6,)), sem((2, reach + 1)), sem((2, ZH)), sem((2, 2, ZH, Y)), sem((2, 2, ZH)),
        sem((2, X)), sem((2, ZL)), sem((2, 2, CHUNKS, X)), sem((2, 2, CHUNKS)),
        sem((2, CHUNKS, 3)), sem((2, CHUNKS)), sem((2, 2, CHUNKS, X)), sem((2, 2)),
        sem((2,)), sem((2, 2, X * Y)), sem((2, nz)),
    ]
    anywhere = pl.BlockSpec(memory_space=pl.ANY)
    whole = pl.BlockSpec(memory_space=pltpu.VMEM)
    shapes = (
        jax.ShapeDtypeStruct((rows, width), BF16),
        jax.ShapeDtypeStruct((rows, width), BF16),
        jax.ShapeDtypeStruct((per, KEY), F32),
        jax.ShapeDtypeStruct((per, KEY), F32),
    )
    results = pl.pallas_call(
        body,
        out_shape=tuple(vm(r.shape, r.dtype) for r in shapes),
        in_specs=[anywhere] * 6,
        out_specs=(whole,) * 4,
        scratch_shapes=scratch,
        compiler_params=pltpu.CompilerParams(
            collective_id=0, has_side_effects=True, vmem_limit_bytes=VMEM_LIMIT
        ),
        cost_estimate=pl.CostEstimate(
            flops=16 * rows * width * KEY, bytes_accessed=8 * rows * width, transcendentals=rows * lanes
        ),
    )(tokens[0, 0], cotangent[0, 0], query_weight.T, key_weight.T, forget_rate[0], resets)
    output, input_grad, grad_query, grad_key = pl.pallas_call(
        publish,
        out_shape=shapes,
        in_specs=[anywhere] * 4,
        out_specs=(anywhere,) * 4,
        scratch_shapes=[sem((4,))], compiler_params=pltpu.CompilerParams(vmem_limit_bytes=16 * 1024 * 1024),
    )(*results)
    return output[None, None], input_grad[None, None], grad_query, grad_key


def solution(mesh):
    placed = (
        P("seg", "dp", None, None),
        P("seg", "dp", None, None),
        P("dp", None),
        P("dp", None),
        P("seg", "dp", None),
        P("seg", "dp"),
    )
    return jax.shard_map(
        local,
        mesh=mesh,
        in_specs=placed,
        out_specs=(
            P("seg", "dp", None, None),
            P("seg", "dp", None, None),
            P(("seg", "dp"), None),
            P(("seg", "dp"), None),
        ),
        check_vma=False,
    )
```

```python
import jax
import jax.numpy as jnp
from jax import lax
from jax.experimental import pallas as pl
from jax.experimental.pallas import tpu as pltpu
from jax.sharding import PartitionSpec as P

ZL, X = 4, 4
Y, ZH, C = 4, 4, 2
CHUNKS = 2
KEY = 64
VMEM_LIMIT = 56 * 1024 * 1024
F32 = jnp.float32
BF16 = jnp.bfloat16
MESH = pl.DeviceIdType.MESH
QUERY, WRITE = 0, 1
FORE, BACK = 0, 1


def dot(a, b, ca, cb):
    return lax.dot_general(a, b, (((ca,), (cb,)), ((), ())), preferred_element_type=F32)


def feature(values):
    return jnp.where(values > 0, values + 1.0, jnp.exp(jnp.minimum(values, 0.0)))


def feature_slope(values):
    return jnp.where(values > 0, 1.0, jnp.exp(jnp.minimum(values, 0.0)))


def body(
    tok_in, cot_in, wq_in, wk_in, rate_in, reset_in,
    out, igrad, gq, gk,
    tok, cot, wq, wk, rate, reset, tt, tsend, w, rt, sin, rin, zt, zs, zm, za, zb, sb, read, feat, slope, bg, bgs,
    gown, hb, r1, fin, r3,
    s_l, s_zs, s_zr, s_y, s_w, s_rx, s_rz, s_in, s_a, s_bs, s_br, s_bk, s_c, s_t, s_xy, s_e,
):
    rows, width = tok.shape
    shard = wq.shape[1]
    wide = width // (CHUNKS * X)
    span = width // (ZL * C)
    per = span // (X * Y * ZH)
    block_width = min(wide, C * shard)
    nz = ZL * ZH
    reach = (ZH - 1) * ZL // 2
    s = lax.axis_index("seg")
    b = lax.axis_index("dp")
    zl, x = s // X, s % X
    y, zh, c = b // (ZH * C), (b // C) % ZH, b % C
    zi = zh * ZL + zl

    def dev(zl=zl, x=x, y=y, zh=zh, c=c):
        return (zl * X + x, (y * ZH + zh) * C + c)

    started = []

    def make(src, dst, send_sem, recv_sem, target):
        return pltpu.make_async_remote_copy(
            src_ref=src, dst_ref=dst, send_sem=send_sem, recv_sem=recv_sem,
            device_id=target, device_id_type=MESH,
        )

    def send(src, dst, sem, at, target):
        copy = make(src, dst, sem.at[(0,) + at], sem.at[(1,) + at], target)
        copy.start()
        started.append(copy)
        return copy

    moves = ((wk_in, wk), (wq_in, wq), (rate_in, rate), (reset_in, reset), (tok_in, tok), (cot_in, cot))
    loads = [pltpu.make_async_copy(src, dst, s_l.at[i]) for i, (src, dst) in enumerate(moves)]
    for copy in loads:
        copy.start()
    za[...] = jnp.zeros_like(za)
    zb[...] = jnp.zeros_like(zb)
    peers = [dev(c=1 - c)]
    peers += [dev(x=(x + k) % X) for k in range(1, X)]
    peers += [dev(y=(y + k) % Y) for k in range(1, Y)]
    peers += [dev(zl=(zl + k) % ZL) for k in range(1, ZL)]
    near = len(peers)
    for o in range(1, ZH):
        peers.append(dev(zl=jnp.where(o * ZL - zl <= reach, 0, ZL - 1), zh=(zh + o) % ZH))
    edge = (zl == 0) | (zl == ZL - 1)
    barrier = pltpu.get_barrier_semaphore()
    for peer in peers[::-1]:
        pl.semaphore_signal(barrier, inc=1, device_id=peer, device_id_type=MESH)
    for copy in loads[:4]:
        copy.wait()
    lanes = pl.ds(pl.multiple_of(c * shard, shard), shard)
    w[QUERY, y, zh, :, lanes] = wq[...]
    w[WRITE, y, zh, :, lanes] = wk[...]
    factor = jnp.exp(-rate[...]) * (1 - reset[...]).astype(F32)
    factor = jnp.concatenate([factor, jnp.zeros_like(factor)], axis=1)
    rt[zl, x] = jnp.broadcast_to(factor, rt.shape[2:])
    pl.semaphore_wait(barrier, near + jnp.where(edge, reach, 0))

    def block(part, o):
        return w.at[part, y, (zh + o) % ZH, :, lanes]

    spread = []
    for part in (WRITE, QUERY):
        for d in range(reach, 0, -1):
            zt_ = (zi + jnp.where(zl == 0, -d, d) + nz) % nz
            o = (d - 1) // ZL + 1
            o = jnp.where(zl == 0, o, ZH - o)
            spread.append(make(
                block(part, 0), block(part, 0), s_zs.at[part, d], s_zr.at[part, o],
                dev(zl=zt_ % ZL, zh=zt_ // ZL),
            ))

    @pl.when(edge)
    def _():
        for copy in spread:
            copy.start()

    def arrive_z(part, o):
        make(block(part, o), block(part, o), s_zs.at[part, 0], s_zr.at[part, o], dev(zh=(zh + 1) % ZH)).wait_recv()

    along_y = {}

    def start_y(part, o):
        along_y[part, o] = [
            send(block(part, o), block(part, o), s_y, (part, o, k), dev(y=(y + k) % Y))
            for k in sorted(range(1, Y), key=lambda k: -min(k, Y - k))
        ]

    to_core = {WRITE: []}

    def start_core(part, o):
        for copy in along_y[part, o]:
            copy.wait_recv()
        column = w.at[part, :, (zh + o) % ZH, :, lanes]
        to_core[part].append(send(column, column, s_w, (part, o), dev(c=1 - c)))

    def left():
        for copy in started:
            copy.wait_send()
        started.clear()

    def left_early():
        left()

        @pl.when(edge)
        def _():
            for copy in spread:
                copy.wait_send()

        for way, j in plan:
            @pl.when(place[way] % 2 == 0)
            def _():
                pass_a(way, j).wait_send()

            @pl.when(place[way] == 1)
            def _():
                pass_b(way, j, 1).wait_send()
                pass_b(way, j, 2).wait_send()

    offsets = sorted(range(1, ZH), key=lambda o: min(o, ZH - o))
    start_y(WRITE, 0)
    own = rt.at[zl, x]
    gotx = [send(own, own, s_rx, (k,), dev(x=(x + k) % X)) for k in range(1, X)]
    loads[4].wait()
    step = width // 8
    for n in range(8):
        piece = tok[:, n * step:(n + 1) * step].astype(F32).T.reshape(step // (C * per), C, per, rows)
        first = piece[:, 0].reshape(step // C, rows)
        second = piece[:, 1].reshape(step // C, rows)
        at = slice(n * step // C, (n + 1) * step // C)
        tt[at, :rows] = jnp.where(c == 0, first, second).astype(BF16)
        tsend[at] = jnp.where(c == 0, second, first).astype(BF16)
    got_tokens = send(tsend, tt.at[:, pl.ds(rows, rows)], s_t, (), dev(c=1 - c))
    for copy in gotx:
        copy.wait_recv()
    own = rt.at[zl]
    gotz = [send(own, own, s_rz, (k,), dev(zl=(zl + k) % ZL)) for k in range(1, ZL)]
    loads[5].wait()
    for o in offsets:
        arrive_z(WRITE, o)
        start_y(WRITE, o)
    for o in [0] + offsets:
        start_core(WRITE, o)
    for o in offsets:
        arrive_z(QUERY, o)
    line = w.at[QUERY, y, :, :, lanes]
    queries_y = [send(line, line, s_y, (QUERY, 0, k), dev(y=(y + k) % Y)) for k in range(1, Y)]
    for copy in to_core[WRITE]:
        copy.wait_recv()

    pairs = [(n // ZH, n % ZH, slice(n * C * shard, (n + 1) * C * shard)) for n in range(Y * ZH)]

    def turned(part):
        total = jnp.zeros((KEY, rows), F32)
        for i, j, at in pairs:
            total = total + dot(w[part, i, j], tok[:, at], 1, 1)
        return feature(total).astype(BF16)

    def straight(part):
        total = jnp.zeros((rows, KEY), F32)
        for i, j, at in pairs:
            total = total + dot(tok[:, at], w[part, i, j], 1, 1)
        feat[part] = feature(total).astype(BF16)
        slope[part] = feature_slope(total)

    ins = {}

    def exchange(way, weights, values, scale):
        for j in range(CHUNKS):
            at = slice(j * X * wide, (j + 1) * X * wide)
            term = (dot(weights, values[:, at], 1, 0) * scale).astype(BF16)
            for q in range(X):
                sin[way, j, q] = term[:, q * wide:(q + 1) * wide]
            ins[way, j] = [
                send(sin.at[way, j, (x + k) % X], rin.at[way, j, x], s_in, (way, j, k), dev(x=(x + k) % X))
                for k in sorted(range(1, X), key=lambda k: -min(k, X - k))
            ]
            rin[way, j, x] = sin[way, j, x]

    exchange(FORE, turned(WRITE), tok, 1.0 / rows)
    straight(WRITE)

    eye = lax.broadcasted_iota(jnp.int32, (KEY, KEY), 0) == lax.broadcasted_iota(jnp.int32, (KEY, KEY), 1)

    def column(row):
        return jnp.sum(jnp.where(eye, row[0:1, :KEY], 0.0), axis=1, keepdims=True)

    for copy in gotz:
        copy.wait_recv()
    keep = [column(rt[zl, i]) for i in range(X)]
    whole = keep[0]
    for i in range(1, X):
        whole = whole * keep[i]
    place = {FORE: zl, BACK: ZL - 1 - zl}
    ahead = {FORE: 1, BACK: -1}
    order = {FORE: list(range(X)), BACK: list(range(X))[::-1]}
    from_a, from_b = {}, {}
    for way, row in ((FORE, ZL - 2), (BACK, 1)):
        skipped = column(rt[row, 0])
        for i in range(1, X):
            skipped = skipped * column(rt[row, i])
        one = jnp.ones_like(skipped)
        p = place[way]
        from_a[way] = jnp.where(p % 2 == 1, one, 0.0)
        from_b[way] = jnp.where(p == 2, one, jnp.where(p == 3, skipped, 0.0))

    for copy in queries_y:
        copy.wait_recv()
    column = w.at[QUERY, :, :, :, lanes]
    send(column, column, s_w, (QUERY, 0), dev(c=1 - c)).wait_recv()
    exchange(BACK, turned(QUERY), cot, 1.0)


    def hop(way, steps):
        return dev(zl=(zl + ahead[way] * steps + ZL) % ZL)

    def pass_a(way, j):
        return make(zs.at[way, j], za.at[way, j], s_a.at[0, way, j], s_a.at[1, way, j], hop(way, 1))

    def pass_b(way, j, n):
        return make(zm.at[way, j], zb.at[way, j], s_bs.at[way, j, n], s_br.at[way, j], hop(way, n))

    def totals(way, j):
        for copy in ins[way, j]:
            copy.wait_recv()
        total = rin[way, j, order[way][0]].astype(F32)
        for i in order[way][1:]:
            total = keep[i] * total + rin[way, j, i].astype(F32)
        zt[way, j] = total
        zs[way, j] = total.astype(BF16)

        @pl.when(place[way] % 2 == 0)
        def _():
            pass_a(way, j).start()

    def relay(way, j):
        @pl.when(place[way] == 1)
        def _():
            pass_a(way, j).wait_recv()
            zm[way, j] = (whole * za[way, j].astype(F32) + zt[way, j]).astype(BF16)
            pass_b(way, j, 1).start()
            pass_b(way, j, 2).start()

    backs = {}

    def finish(way, j):
        @pl.when(place[way] >= 2)
        def _():
            pass_b(way, j, 1).wait_recv()

        @pl.when(place[way] == 3)
        def _():
            pass_a(way, j).wait_recv()

        state = from_a[way] * za[way, j].astype(F32) + from_b[way] * zb[way, j].astype(F32)
        for n, i in enumerate(order[way]):
            sb[way, j, i] = state.astype(BF16)
            if n < X - 1:
                state = keep[i] * state + rin[way, j, i].astype(F32)
        backs[way, j] = [
            send(sb.at[way, j, (x + k) % X], read.at[way, j, x], s_bk, (way, j, k), dev(x=(x + k) % X))
            for k in sorted(range(1, X), key=lambda k: -min(k, X - k))
        ]
        read[way, j, x] = sb[way, j, x]

    plan = [(way, j) for way in (FORE, BACK) for j in range(CHUNKS)]
    for n in range(len(plan) + 2):
        if n < len(plan):
            totals(*plan[n])
        if 1 <= n <= len(plan):
            relay(*plan[n - 1])
        if n >= 2:
            finish(*plan[n - 2])
    straight(QUERY)

    half = ZL // 2
    blank = jnp.zeros((C * rows, KEY), BF16)
    other, plane = {}, {}
    got_tokens.wait_recv()

    def against(way, values, js):
        total = jnp.zeros((rows, KEY), F32)
        for j in js:
            for copy in backs[way, j]:
                copy.wait_recv()
            for q in range(X):
                at = slice((j * X + q) * wide, (j * X + q + 1) * wide)
                total = total + dot(values[:, at], read[way, j, q], 1, 1)
        return total

    def share(part, grad):
        bg[part] = grad
        other[part] = send(bg.at[part], bgs.at[part], s_c, (part,), dev(c=1 - c))

    def over_plane(part):
        other[part].wait_recv()
        grads = jnp.concatenate([bg[part], bgs[part]], axis=0)
        low = jnp.concatenate([grads, blank], axis=1)
        high = jnp.concatenate([blank, grads], axis=1)
        for z in range(half):
            g = dot(tt[z * span:(z + 1) * span], low, 1, 0)
            g = g + dot(tt[(z + half) * span:(z + half + 1) * span], high, 1, 0)
            g = g.reshape(X, Y, ZH * per, 2 * KEY)
            gown[part, z] = g
            hb[part, z] = g.astype(BF16)
        plane[part] = []
        for k in sorted(range(1, X * Y), key=lambda k: -min(k // Y, X - k // Y) - min(k % Y, Y - k % Y)):
            xt, yt = (x + k // Y) % X, (y + k % Y) % Y
            plane[part].append(send(hb.at[part, :, xt, yt], r1.at[part, k], s_xy, (part, k), dev(x=xt, y=yt)))

    def gather_plane(part):
        for copy in plane[part]:
            copy.wait_recv()
        total = gown[part, :, x, y]
        for k in range(1, X * Y):
            total = total + r1[part, k].astype(F32)
        for h in range(2):
            piece = total[:, :, h * KEY:(h + 1) * KEY].reshape(half, ZH, per, KEY)
            fin[h * half:(h + 1) * half, :, :, part * KEY:(part + 1) * KEY] = piece

    query_grad = (against(FORE, cot, range(CHUNKS)) * slope[QUERY]).astype(BF16)
    share(QUERY, query_grad)
    over_plane(QUERY)
    wanted = against(BACK, tok, range(CHUNKS - 1))
    wanted = wanted + against(BACK, tok, range(CHUNKS - 1, CHUNKS))
    key_grad = (wanted / rows * slope[WRITE]).astype(BF16)
    share(WRITE, key_grad)
    over_plane(WRITE)

    for j in range(CHUNKS):
        for q in range(X):
            at = slice((j * X + q) * wide, (j * X + q + 1) * wide)
            out[:, at] = (tok[:, at].astype(F32) + dot(feat[QUERY], read[FORE, j, q], 1, 0)).astype(BF16)
    early = started[:]
    started[:] = [copy for copy in early if not any(copy is other for part in plane for other in plane[part])]
    kept = [copy for copy in early if not any(copy is other for other in started)]
    left_early()
    gather_plane(QUERY)
    gather_plane(WRITE)
    last = []
    for k in sorted(range(1, nz), key=lambda k: -min(k, nz - k)):
        zt_ = (zi + k) % nz
        last.append(send(fin.at[zt_ % ZL, zt_ // ZL], r3.at[k], s_e, (k,), dev(zl=zt_ % ZL, zh=zt_ // ZL)))

    for n in range(0, width, block_width):
        at = slice(n, n + block_width)
        j, q, k = n // (X * wide), n // wide % X, n % wide
        i, m, n = n // (ZH * C * shard), n // (C * shard) % ZH, n % (C * shard)
        total = cot[:, at].astype(F32) + dot(feat[WRITE], read[BACK, j, q, :, k:k + block_width], 1, 0) / rows
        for part in (QUERY, WRITE):
            total = total + dot(bg[part], w[part, i, m, :, n:n + block_width], 1, 0)
        igrad[:, at] = total.astype(BF16)
    for copy in kept:
        copy.wait_send()
    for copy in last:
        copy.wait_recv()
    total = fin[zl, zh]
    for k in range(1, nz):
        total = total + r3[k]
    gq[...] = total[:, :KEY]
    gk[...] = total[:, KEY:]

    left()


def publish(*refs):
    copies = [pltpu.make_async_copy(refs[i], refs[4 + i], refs[8].at[i]) for i in range(4)]
    for copy in copies:
        copy.start()
    for copy in copies:
        copy.wait()


def local(tokens, cotangent, query_weight, key_weight, forget_rate, resets):
    rows, width = tokens.shape[2:]
    shard = query_weight.shape[0]
    wide = width // (CHUNKS * X)
    half = ZL // 2
    span = width // ZL
    per = span // (X * Y * ZH * C)
    nz = ZL * ZH
    reach = (ZH - 1) * ZL // 2
    lanes = 2 * KEY
    vm = pltpu.VMEM
    sem = pltpu.SemaphoreType.DMA
    scratch = [
        vm((rows, width), BF16),
        vm((rows, width), BF16),
        vm((KEY, shard), BF16),
        vm((KEY, shard), BF16),
        vm((1, KEY), F32),
        vm((1, 1), jnp.int32),
        vm((width // C, C * rows), BF16),
        vm((width // C, rows), BF16),
        vm((2, Y, ZH, KEY, C * shard), BF16),
        vm((ZL, X, 8, lanes), F32),
        vm((2, CHUNKS, X, KEY, wide), BF16),
        vm((2, CHUNKS, X, KEY, wide), BF16),
        vm((2, CHUNKS, KEY, wide), F32),
        vm((2, CHUNKS, KEY, wide), BF16),
        vm((2, CHUNKS, KEY, wide), BF16),
        vm((2, CHUNKS, KEY, wide), BF16),
        vm((2, CHUNKS, KEY, wide), BF16),
        vm((2, CHUNKS, X, KEY, wide), BF16),
        vm((2, CHUNKS, X, KEY, wide), BF16),
        vm((2, rows, KEY), BF16),
        vm((2, rows, KEY), F32),
        vm((2, rows, KEY), BF16),
        vm((2, rows, KEY), BF16),
        vm((2, half, X, Y, ZH * per, lanes), F32),
        vm((2, half, X, Y, ZH * per, lanes), BF16),
        vm((2, X * Y, half, ZH * per, lanes), BF16),
        vm((ZL, ZH, per, lanes), F32),
        vm((nz, per, lanes), F32),
        sem((6,)), sem((2, reach + 1)), sem((2, ZH)), sem((2, 2, ZH, Y)), sem((2, 2, ZH)),
        sem((2, X)), sem((2, ZL)), sem((2, 2, CHUNKS, X)), sem((2, 2, CHUNKS)),
        sem((2, CHUNKS, 3)), sem((2, CHUNKS)), sem((2, 2, CHUNKS, X)), sem((2, 2)),
        sem((2,)), sem((2, 2, X * Y)), sem((2, nz)),
    ]
    anywhere = pl.BlockSpec(memory_space=pl.ANY)
    whole = pl.BlockSpec(memory_space=pltpu.VMEM)
    shapes = (
        jax.ShapeDtypeStruct((rows, width), BF16),
        jax.ShapeDtypeStruct((rows, width), BF16),
        jax.ShapeDtypeStruct((per, KEY), F32),
        jax.ShapeDtypeStruct((per, KEY), F32),
    )
    results = pl.pallas_call(
        body,
        out_shape=tuple(vm(r.shape, r.dtype) for r in shapes),
        in_specs=[anywhere] * 6,
        out_specs=(whole,) * 4,
        scratch_shapes=scratch,
        compiler_params=pltpu.CompilerParams(
            collective_id=0, has_side_effects=True, vmem_limit_bytes=VMEM_LIMIT
        ),
        cost_estimate=pl.CostEstimate(
            flops=16 * rows * width * KEY, bytes_accessed=8 * rows * width, transcendentals=rows * lanes
        ),
    )(tokens[0, 0], cotangent[0, 0], query_weight.T, key_weight.T, forget_rate[0], resets)
    output, input_grad, grad_query, grad_key = pl.pallas_call(
        publish,
        out_shape=shapes,
        in_specs=[anywhere] * 4,
        out_specs=(anywhere,) * 4,
        scratch_shapes=[sem((4,))], compiler_params=pltpu.CompilerParams(vmem_limit_bytes=16 * 1024 * 1024),
    )(*results)
    return output[None, None], input_grad[None, None], grad_query, grad_key


def solution(mesh):
    placed = (
        P("seg", "dp", None, None),
        P("seg", "dp", None, None),
        P("dp", None),
        P("dp", None),
        P("seg", "dp", None),
        P("seg", "dp"),
    )
    return jax.shard_map(
        local,
        mesh=mesh,
        in_specs=placed,
        out_specs=(
            P("seg", "dp", None, None),
            P("seg", "dp", None, None),
            P(("seg", "dp"), None),
            P(("seg", "dp"), None),
        ),
        check_vma=False,
    )
```
